256 devices in a mesh: dp: 4 (over y), expert: 64 (over x, z, core).
Axes of the slice: x: 4, y: 4, z: 8, core: 2. Of those that a mesh axis runs over, the one named last changes fastest.
Arguments:
- tokens: bfloat16 [8192, 3584], P('expert', 'dp'), may hold values from -6 to 6
- grad_out: bfloat16 [8192, 3584], P('expert', 'dp'), may hold values from -1.5 to 1.5
- routes: int32 [8192, 2], P('expert'), may hold values from 0 to 63, all different within a row; in each aligned block of 128 rows (0 to 127, 128 to 255, ...) at most 8 rows name the same one
- gates: bfloat16 [8192, 2], P('expert'), may hold values from 0.19921875 to 1
- replicated: int32 [64], P('expert'), may hold values from 0 to 1, as said below
- w_gate: bfloat16 [64, 3584, 1024], P('expert', None, 'dp'), as said below
- w_up: bfloat16 [64, 3584, 1024], P('expert', None, 'dp'), as said below
- w_down: bfloat16 [64, 1024, 3584], P('expert', 'dp'), as said below
Outputs:
- grad_tokens: bfloat16 [8192, 3584], P('expert', 'dp')
- grad_gate: bfloat16 [64, 3584, 1024], P('expert', None, 'dp')
- grad_up: bfloat16 [64, 3584, 1024], P('expert', None, 'dp')
- grad_down: bfloat16 [64, 1024, 3584], P('expert', 'dp')
The draws below stay inside these ranges and needn't reach their ends.
Inputs may be any that keep to these rules, and one draw needn't show every extreme that they name: `routes`: A token names 2 different slots. Among the entries of the tokens of one index of expert (aligned blocks of 128 rows) no slot is named more than 8 times, a bound that some block reaches. `replicated`: equal in the two slots 2j and 2j + 1 of a pair; one to all but one of the 32 pairs hold 1. `w_gate`: the two slots of a pair with replicated 1 hold equal weights. `w_up`: the two slots of a pair with replicated 1 hold equal weights. `w_down`: the two slots of a pair with replicated 1 hold equal weights.
All inputs are finite; a program needn't handle non-finite values.
Results may differ from the reference program's by a relative error of at most 0.0054.
Values may be sent and summed in bfloat16 or wider, within the bound.
A program may use at most 128 MiB of HBM per device.

```python
import math
import jax
import jax.numpy as jnp
import numpy as np
from jax import lax

D = 3584
H = 1024
TOPK = 2
TOK_DEV = 128
SLOTS = 64
CAP = 8
TOKENS = 8192


def pair_flags(key):
    pair_count = SLOTS // 2
    count_key = jax.random.fold_in(key, 7)
    order_key = jax.random.fold_in(key, 11)
    chosen = jax.random.randint(count_key, (), 1, pair_count)
    shuffled = jax.random.permutation(order_key, pair_count)
    return shuffled < chosen


def mirrored(values, replica_flags):
    paired = values.reshape((SLOTS // 2, 2) + values.shape[1:])
    first_copy = paired[:, :1]
    pair_mask = replica_flags.reshape((SLOTS // 2, 1) + (1,) * (values.ndim - 1))
    mirrored_pairs = jnp.where(pair_mask, jnp.concatenate([first_copy, first_copy], axis=1), paired)
    return mirrored_pairs.reshape(values.shape)


def draw_replicated(key, part):
    replica_flags = pair_flags(key)
    return jnp.repeat(replica_flags.astype(jnp.int32), 2)


def draw_w_gate(key, part):
    replica_flags = pair_flags(key)
    key = jax.random.fold_in(key, 21)
    values = jax.random.normal(key, (SLOTS, D, H), jnp.float32) * (1.0 / math.sqrt(D))
    return mirrored(values, replica_flags).astype(jnp.bfloat16)


def draw_w_up(key, part):
    replica_flags = pair_flags(key)
    key = jax.random.fold_in(key, 22)
    values = jax.random.normal(key, (SLOTS, D, H), jnp.float32) * (1.0 / math.sqrt(D))
    return mirrored(values, replica_flags).astype(jnp.bfloat16)


def draw_w_down(key, part):
    replica_flags = pair_flags(key)
    key = jax.random.fold_in(key, 23)
    values = jax.random.normal(key, (SLOTS, H, D), jnp.float32) * (1.0 / math.sqrt(H))
    return mirrored(values, replica_flags).astype(jnp.bfloat16)


def block_scale(own_key, dims, pieces, low, high):
    factor_of = 1.0
    for position, parts in pieces:
        heights = jax.random.uniform(jax.random.fold_in(jax.random.fold_in(own_key, 6), position), (parts,), jnp.float32, low / len(pieces), high / len(pieces))
        factor_of = factor_of * jnp.repeat(jnp.exp(heights), dims[position] // parts).reshape((-1,) + (1,) * (len(dims) - 1 - position))
    return factor_of


def deal_out(stream_key, own, number, rows, amount, top, reach, slope):
    ranking = jax.random.permutation(stream_key, amount)
    packed, ordinary = portions_of(amount, rows * top, reach, slope, True), portions_of(amount, rows * top, reach, slope, False)
    places = jnp.arange(amount)

    def named(tallies, rotation):
        used = int((tallies > 0).sum())
        fixed = max(1, used // 4)
        shifted = fixed + (places - fixed + rotation * (used - fixed)) % max(1, amount - fixed)
        return jnp.zeros((amount,), jnp.int32).at[ranking[jnp.where(places < fixed, places, shifted)]].set(jnp.asarray(tallies, jnp.int32))

    tallies = jnp.where(number % 4 == 0, named(packed, number // 4), named(ordinary, number - number // 4 - 1))
    mixed = jax.random.permutation(jax.random.fold_in(own, 3), amount)
    source_of, sink = mixed[0:amount // 2 * 2:2], mixed[1:amount // 2 * 2:2]
    room = jnp.minimum(tallies[source_of] - 1, reach - tallies[sink]) // 2
    room = jnp.where((source_of == ranking[0]) | (sink == ranking[0]) | (tallies[sink] == 0), 0, jnp.maximum(room, 0))
    shifted = jax.random.randint(jax.random.fold_in(own, 4), (amount // 2,), 0, 1 << 20) % (room + 1)
    tallies = tallies.at[source_of].add(-shifted).at[sink].add(shifted)
    labels = jnp.searchsorted(jnp.cumsum(tallies), jnp.arange(rows * top), side="right").astype(jnp.int32)
    listing = labels.reshape(top, rows).T
    listing = listing[jax.random.permutation(jax.random.fold_in(own, 1), rows)]
    rotation = jax.random.randint(jax.random.fold_in(own, 2), (rows, 1), 0, top)
    return jnp.take_along_axis(listing, (jnp.arange(top)[None, :] + rotation) % top, axis=1)


def portions_of(number_of, total, bound, skew, full):
    portions = [(1 << 20) // math.isqrt(grade ** skew) + 1 for grade in range(1, number_of + 1)]
    largest = bound if full else min(bound, max(-(-total // number_of), total * portions[0] // sum(portions)))
    least = 1 if total - largest >= number_of - 1 else 0
    holding, surplus = [largest] + [least] * (number_of - 1), total - largest - least * (number_of - 1)
    while surplus > 0:
        free = [i for i in range(1, number_of) if holding[i] < largest] or [i for i in range(1, number_of) if holding[i] < bound]
        mass, budget = sum([portions[i] for i in free]), surplus
        for i in free:
            more = min(bound - holding[i], max(1, budget * portions[i] // mass), surplus)
            holding[i] = holding[i] + more
            surplus = surplus - more
    return np.array(holding)


def bell_draw(own_key, shape, deviation, bound, cuts=(), held_as=jnp.bfloat16):
    result = deviation * jax.random.normal(own_key, shape, jnp.float32)
    if cuts:
        result = result * block_scale(own_key, shape, cuts, -0.22, 0.18)
    return jnp.clip(result, -bound, bound).astype(held_as)


def setup_inputs(seed: int = 0) -> dict:
    splits = jax.random.split(jax.random.key(seed), 9)
    tokens = bell_draw(splits[0], (TOKENS, D), 1.0, 6.0, ((0, 64), (1, 4)))
    grad_out = bell_draw(splits[1], (TOKENS, D), 0.25, 1.5, ((0, 64), (1, 4)))
    routes_keys = jax.random.split(jax.random.fold_in(splits[2], 1), TOKENS // TOK_DEV)
    routes_turns = jax.random.permutation(jax.random.fold_in(splits[2], 3), TOKENS // TOK_DEV)
    routes = jax.vmap(lambda own, number: deal_out(jax.random.fold_in(splits[2], 2), own, number, TOK_DEV, SLOTS, TOPK, CAP, 2))(routes_keys, routes_turns).reshape((TOKENS, TOPK))
    gates = jnp.clip(0.19921875 + 0.80078125 * jax.random.uniform(splits[3], (TOKENS, TOPK), jnp.float32) ** block_scale(splits[3], (TOKENS, TOPK), ((0, 64),), -0.2, 0.2), 0.19921875, 1.0).astype(jnp.bfloat16)
    replicated = draw_replicated(jax.random.fold_in(splits[8], 71), 0)
    w_gate = draw_w_gate(jax.random.fold_in(splits[8], 71), 0)
    w_up = draw_w_up(jax.random.fold_in(splits[8], 71), 0)
    w_down = draw_w_down(jax.random.fold_in(splits[8], 71), 0)
    return dict(tokens=tokens, grad_out=grad_out, routes=routes, gates=gates, replicated=replicated, w_gate=w_gate, w_up=w_up, w_down=w_down)


def expert_backward(x_rows, dy_rows, gate_col, weight_gate, weight_up, weight_down):
    pre_gate = jnp.dot(x_rows, weight_gate, preferred_element_type=jnp.float32)
    pre_up = jnp.dot(x_rows, weight_up, preferred_element_type=jnp.float32)
    sigmoid_v = jax.nn.sigmoid(pre_gate)
    activated = pre_gate * sigmoid_v
    scaled_hidden = (gate_col * activated * pre_up).astype(jnp.bfloat16)
    d_hidden = gate_col * lax.dot_general(dy_rows, weight_down, (((1,), (1,)), ((), ())), preferred_element_type=jnp.float32)
    d_up = (d_hidden * activated).astype(jnp.bfloat16)
    d_gate = (d_hidden * pre_up * sigmoid_v * (1.0 + pre_gate * (1.0 - sigmoid_v))).astype(jnp.bfloat16)
    grad_gate = lax.dot_general(x_rows, d_gate, (((0,), (0,)), ((), ())), preferred_element_type=jnp.float32)
    grad_up = lax.dot_general(x_rows, d_up, (((0,), (0,)), ((), ())), preferred_element_type=jnp.float32)
    grad_down = lax.dot_general(scaled_hidden, dy_rows, (((0,), (0,)), ((), ())), preferred_element_type=jnp.float32)
    d_rows = lax.dot_general(d_gate, weight_gate, (((1,), (1,)), ((), ())), preferred_element_type=jnp.float32)
    d_rows = d_rows + lax.dot_general(d_up, weight_up, (((1,), (1,)), ((), ())), preferred_element_type=jnp.float32)
    return d_rows, grad_gate, grad_up, grad_down


def pair_sum(partials, replicated):
    shape_all = partials.shape
    paired = partials.reshape((SLOTS // 2, 2) + shape_all[1:])
    swapped = paired[:, ::-1].reshape(shape_all)
    added = (partials.astype(jnp.float32) + swapped.astype(jnp.float32)).astype(jnp.bfloat16)
    replica_flag = (replicated == 1).reshape((SLOTS, 1, 1))
    return jnp.where(replica_flag, added, partials)


def reference(tokens, grad_out, routes, gates, replicated, w_gate, w_up, w_down):
    flat_routes = routes.reshape(-1)
    pair_total = flat_routes.shape[0]
    buffer_rows = SLOTS * CAP
    token_ids = (jnp.arange(pair_total, dtype=jnp.int32) // TOPK).astype(jnp.int32)
    flat_gates = gates.reshape(-1).astype(jnp.float32)

    def one_slot(running, slot_index):
        is_other = jnp.where(flat_routes == slot_index, 0, 1).astype(jnp.int32)
        ordering = jnp.argsort(is_other, stable=True)[:buffer_rows]
        is_live = is_other[ordering] == 0
        row_ids = token_ids[ordering]
        x_rows = jnp.where(is_live[:, None], tokens[row_ids], jnp.zeros((), tokens.dtype))
        dy_rows = jnp.where(is_live[:, None], grad_out[row_ids], jnp.zeros((), grad_out.dtype))
        gate_col = jnp.where(is_live, flat_gates[ordering], jnp.zeros((), jnp.float32))[:, None]
        d_rows, grad_gate, grad_up, grad_down = expert_backward(
            x_rows, dy_rows, gate_col, w_gate[slot_index], w_up[slot_index], w_down[slot_index])
        running = running.at[row_ids].add(jnp.where(is_live[:, None], d_rows, jnp.zeros((), jnp.float32)))
        return running, (grad_gate.astype(jnp.bfloat16), grad_up.astype(jnp.bfloat16), grad_down.astype(jnp.bfloat16))

    start = jnp.zeros((TOKENS, D), jnp.float32)
    summed, partials = lax.scan(one_slot, start, jnp.arange(SLOTS, dtype=jnp.int32))
    grad_tokens = summed.astype(jnp.bfloat16)
    return (grad_tokens, pair_sum(partials[0], replicated), pair_sum(partials[1], replicated),
            pair_sum(partials[2], replicated))
```

```python
import functools

import jax
import jax.numpy as jnp
from jax import lax
from jax.experimental import pallas as pl
from jax.experimental.pallas import tpu as pltpu
from jax.sharding import PartitionSpec as P

MESH = pl.DeviceIdType.MESH
BF, F32 = jnp.bfloat16, jnp.float32
D, H, DP = 3584, 1024, 4
FQ, HQ = D // DP, H // DP
TOK, CAP, SLOTS = 128, 8, 64
NX, NZ = 4, 8
NCH = 8
NPAIR = 4
MSG = FQ + 128
RET = 512


def z_step(j):
    return ((j + 1) // 2) * (1 if j % 2 else -1)


OFFSETS = [(dx, z_step(j) % NZ, dc) for dx in (0, 1, 3, 2) for j in range(NZ) for dc in (0, 1)]
BACK = [OFFSETS.index(((-dx) % NX, (-dz) % NZ, dc)) for dx, dz, dc in OFFSETS]


def dot(a, b, dims):
    return lax.dot_general(a, b, ((dims[0], dims[1]), ((), ())), preferred_element_type=F32)


NN, NT, TN = ((1,), (0,)), ((1,), (1,)), ((0,), (0,))


def kernel(
    tok_ref, dy_ref, routes_ref, gates_ref, flag_ref, wg_ref, wu_ref, wd_ref,
    ret_ref, sel_ref, og_ref, ou_ref, od_ref,
    wgu, wdn, sel, msg, land, rows, gcol, dgu, sh,
    rs_snd, rs_a, rs_b, p_up, p_dn, p_own, fin_snd, fin_rcv, rt_snd, rt_rcv,
    gu_mine, gd_mine, gu_theirs, gd_theirs,
    w_sem, loc_sem, a_snd, a_rcv, y_snd, y_rcv, r_snd, r_rcv, q_snd, q_rcv, f_snd, f_rcv,
    b_snd, b_rcv, g_snd, g_rcv, o_sem,
):
    d = lax.axis_index("dp")
    e = lax.axis_index("expert")
    x0, z0, c0 = e // 16, (e // 2) % NZ, e % 2
    up, dn, op = (d + 1) % DP, (d + 3) % DP, (d + 2) % DP

    def peer(o):
        dx, dz, dc = OFFSETS[o]
        return ((x0 + dx) % NX * NZ + (z0 + dz) % NZ) * 2 + (c0 + dc) % 2

    def remote(src, dst, s, r, dev):
        return pltpu.make_async_remote_copy(src, dst, s, r, device_id=dev, device_id_type=MESH)

    weights_in = [
        pltpu.make_async_copy(wg_ref.at[0], wgu.at[:, pl.ds(0, HQ)], w_sem.at[0]),
        pltpu.make_async_copy(wu_ref.at[0], wgu.at[:, pl.ds(HQ, HQ)], w_sem.at[1]),
        pltpu.make_async_copy(wd_ref.at[0], wdn, w_sem.at[2]),
    ]
    for c in weights_in:
        c.start()

    barrier = pltpu.get_barrier_semaphore()
    for o in range(1, SLOTS):
        pl.semaphore_signal(barrier, inc=1, device_id=(d, peer(o)), device_id_type=MESH)
    for q in range(1, DP):
        pl.semaphore_signal(barrier, inc=1, device_id=((d + q) % DP, e), device_id_type=MESH)

    io = lax.broadcasted_iota(jnp.int32, (SLOTS, TOK), 0)
    dxi = io >> 4
    j = (io >> 1) & 7
    mag = (j + 1) >> 1
    slot_x = (x0 + (dxi ^ (dxi >> 1))) & (NX - 1)
    slot_z = (z0 + jnp.where((j & 1) == 1, mag, -mag)) & (NZ - 1)
    slot = (slot_x * NZ + slot_z) * 2 + (c0 ^ (io & 1))
    on0 = routes_ref[0:1, :] == slot
    on1 = routes_ref[1:2, :] == slot
    hot0 = on0.astype(F32)
    hot1 = on1.astype(F32)
    before = (
        lax.broadcasted_iota(jnp.int32, (TOK, TOK), 0) < lax.broadcasted_iota(jnp.int32, (TOK, TOK), 1)
    ).astype(BF)
    rank0 = dot(hot0.astype(BF), before, NN)
    rank1 = dot(hot1.astype(BF), before, NN) + jnp.sum(hot0, axis=1, keepdims=True)
    rank0 = jnp.where(on0, rank0, -1.0).astype(BF)
    rank1 = jnp.where(on1, rank1, -1.0).astype(BF)
    n_rows = SLOTS * CAP
    ui = lax.broadcasted_iota(jnp.int32, (n_rows, SLOTS), 0)
    spread = ((ui >> 3) == lax.broadcasted_iota(jnp.int32, (n_rows, SLOTS), 1)).astype(BF)
    place = (lax.broadcasted_iota(jnp.int32, (n_rows, TOK), 0) & 7).astype(F32)
    sel0 = (dot(spread, rank0, NN) == place).astype(F32)
    sel1 = (dot(spread, rank1, NN) == place).astype(F32)
    sel[...] = (sel0 + sel1).astype(BF)
    gate_of = (sel0 * gates_ref[0:1, :] + sel1 * gates_ref[1:2, :]).astype(BF)
    gcol[...] = dot(gate_of, jnp.ones((TOK, 128), BF), NN)

    a2a = {}
    for k in range(NCH):
        s = sel[k * 64:(k + 1) * 64, :]
        xk = dot(s, tok_ref[...], NN).reshape(8, 8, FQ)
        yk = dot(s, dy_ref[...], NN).reshape(8, 8, FQ)
        gk = gcol[k * 64:(k + 1) * 64, :].reshape(8, 8, 128)
        msg[k * 8:(k + 1) * 8, :, 0:FQ] = jnp.concatenate([xk, yk], axis=1).astype(BF)
        msg[k * 8:(k + 1) * 8, :, FQ:MSG] = jnp.concatenate([gk, gk], axis=1).astype(BF)
        if k == 0:
            pl.semaphore_wait(barrier, SLOTS - 1 + DP - 1)
            own = pltpu.make_async_copy(msg.at[0], land.at[0], loc_sem.at[0])
            own.start()
        for o in range(max(1, 8 * k), 8 * k + 8):
            a2a[o] = remote(msg.at[o], land.at[o], a_snd.at[k], a_rcv.at[k], (d, peer(o)))
            a2a[o].start()

    def chunk_wait(buf, k, sem, per=8):
        lo = max(1, per * k)
        block = buf.at[pl.ds(lo, per * k + per - lo)]
        pltpu.make_async_copy(block, block, sem.at[k]).wait()

    to_up, to_dn, rel_up, rel_dn = {}, {}, {}, {}

    def forward(k):
        if k == 0:
            own.wait()
        chunk_wait(land, k, a_rcv)
        block = land[k * 8:(k + 1) * 8].astype(F32)
        rows[k, d, 0:64, :] = block[:, 0:8, 0:FQ].reshape(64, FQ).astype(BF)
        rows[k, d, 64:128, :] = block[:, 8:16, 0:FQ].reshape(64, FQ).astype(BF)
        gcol[k * 64:(k + 1) * 64, :] = block[:, 0:8, FQ:MSG].reshape(64, 128)
        mine = rows.at[k, d]
        to_up[k] = remote(mine, mine, y_snd.at[k, 0], y_rcv.at[k, 0], (up, e))
        to_dn[k] = remote(mine, mine, y_snd.at[k, 1], y_rcv.at[k, 1], (dn, e))
        to_up[k].start()
        to_dn[k].start()

    def relay(k):
        to_up[k].wait_recv()
        part = rows.at[k, dn, pl.ds(0, 64)]
        rel_up[k] = remote(part, part, r_snd.at[k, 0], r_rcv.at[k, 0], (up, e))
        rel_up[k].start()
        to_dn[k].wait_recv()
        part = rows.at[k, up, pl.ds(64, 64)]
        rel_dn[k] = remote(part, part, r_snd.at[k, 1], r_rcv.at[k, 1], (dn, e))
        rel_dn[k].start()

    def row_part(p, q):
        rng = pl.ds(pl.multiple_of(q * FQ, FQ), FQ)
        return dot(dgu[p * 128:(p + 1) * 128, :], wgu[rng, :], NT)

    rs_c = {}

    def compute(p):
        for k in (2 * p, 2 * p + 1):
            rel_up[k].wait_recv()
            rel_dn[k].wait_recv()
        pre = jnp.zeros((128, 2 * HQ), F32)
        dh = jnp.zeros((128, HQ), F32)
        for q in range(DP):
            xq = rows[2 * p:2 * p + 2, q, 0:64, :].reshape(128, FQ)
            yq = rows[2 * p:2 * p + 2, q, 64:128, :].reshape(128, FQ)
            pre = pre + dot(xq, wgu[q * FQ:(q + 1) * FQ, :], NN)
            dh = dh + dot(yq, wdn[:, q * FQ:(q + 1) * FQ], NT)
        g = gcol[p * 128:(p + 1) * 128, :]
        g = jnp.concatenate([g, g], axis=1)
        pg, pu = pre[:, 0:HQ], pre[:, HQ:]
        sig = jax.nn.sigmoid(pg)
        act = pg * sig
        dh = g * dh
        span = slice(p * 128, (p + 1) * 128)
        sh[span, :] = (g * act * pu).astype(BF)
        dgu[span, 0:HQ] = (dh * pu * sig * (1.0 + pg * (1.0 - sig))).astype(BF)
        dgu[span, HQ:] = (dh * act).astype(BF)
        rs_snd[p] = row_part(p, op).astype(BF)
        rs_c[p] = (
            remote(rs_snd.at[p, pl.ds(0, 64)], rs_a.at[p], q_snd.at[p, 0], q_rcv.at[p, 0], (up, e)),
            remote(rs_snd.at[p, pl.ds(64, 64)], rs_b.at[p], q_snd.at[p, 1], q_rcv.at[p, 1], (dn, e)),
        )
        for c in rs_c[p]:
            c.start()
        p_up[p] = row_part(p, up)
        p_dn[p] = row_part(p, dn)
        p_own[p] = row_part(p, d)

    fin_c = {}

    def stage2(p):
        rs_c[p][0].wait_recv()
        fin_snd[p, 0, 0:64, :] = (p_up[p, 0:64, :] + rs_a[p].astype(F32)).astype(BF)
        fin_snd[p, 0, 64:128, :] = p_up[p, 64:128, :].astype(BF)
        first = remote(fin_snd.at[p, 0], fin_rcv.at[p, 0], f_snd.at[p, 0], f_rcv.at[p, 0], (up, e))
        first.start()
        rs_c[p][1].wait_recv()
        fin_snd[p, 1, 0:64, :] = p_dn[p, 0:64, :].astype(BF)
        fin_snd[p, 1, 64:128, :] = (p_dn[p, 64:128, :] + rs_b[p].astype(F32)).astype(BF)
        second = remote(fin_snd.at[p, 1], fin_rcv.at[p, 1], f_snd.at[p, 1], f_rcv.at[p, 1], (dn, e))
        second.start()
        fin_c[p] = (first, second)

    back_c = {}

    def stage3(p):
        fin_c[p][0].wait_recv()
        fin_c[p][1].wait_recv()
        total = p_own[p] + fin_rcv[p, 0].astype(F32) + fin_rcv[p, 1].astype(F32)
        total = total.reshape(16, 8, FQ)
        tail = jnp.concatenate([total[:, :, RET:FQ], jnp.zeros((16, 8, 2 * RET - FQ), F32)], axis=2)
        rt_snd[16 * p:16 * p + 16] = jnp.concatenate([total[:, :, 0:RET], tail], axis=1).astype(BF)
        if p == 0:
            pltpu.make_async_copy(rt_snd.at[0], rt_rcv.at[0], loc_sem.at[1]).start()
        for o in range(max(1, 16 * p), 16 * p + 16):
            back_c[o] = remote(rt_snd.at[o], rt_rcv.at[o], b_snd.at[p], b_rcv.at[p], (d, peer(BACK[o])))
            back_c[o].start()

    pair_c = []
    partner = (d, e + 1 - 2 * c0)

    def weight_grads(q):
        xq = rows[:, q, 0:64, :].reshape(n_rows, FQ)
        gu_mine[q * FQ:(q + 1) * FQ, :] = dot(xq, dgu[...], TN).astype(BF)
        part = pl.ds(q * FQ, FQ)
        c = remote(gu_mine.at[part], gu_theirs.at[part], g_snd.at[q, 0], g_rcv.at[q, 0], partner)
        c.start()
        pair_c.append(c)
        yq = rows[:, q, 64:128, :].reshape(n_rows, FQ)
        gd_mine[q] = dot(sh[...], yq, TN).astype(BF)
        c = remote(gd_mine.at[q], gd_theirs.at[q], g_snd.at[q, 1], g_rcv.at[q, 1], partner)
        c.start()
        pair_c.append(c)

    out_c = []

    def merge(q):
        replica = flag_ref[...] == 1
        part = pl.ds(q * FQ, FQ)
        pair_c[2 * q].wait_recv()
        mine = gu_mine[q * FQ:(q + 1) * FQ, :].astype(F32)
        theirs = gu_theirs[q * FQ:(q + 1) * FQ, :].astype(F32)
        gu_theirs[q * FQ:(q + 1) * FQ, :] = (mine + jnp.where(replica, theirs, 0.0)).astype(BF)
        pair_c[2 * q + 1].wait_recv()
        mine = gd_mine[q].astype(F32)
        theirs = gd_theirs[q].astype(F32)
        gd_theirs[q] = (mine + jnp.where(replica, theirs, 0.0)).astype(BF)
        copies = (
            pltpu.make_async_copy(gu_theirs.at[part, pl.ds(0, HQ)], og_ref.at[0, part], o_sem.at[q, 0]),
            pltpu.make_async_copy(gu_theirs.at[part, pl.ds(HQ, HQ)], ou_ref.at[0, part], o_sem.at[q, 1]),
            pltpu.make_async_copy(gd_theirs.at[q], od_ref.at[0, :, part], o_sem.at[q, 2]),
        )
        for c in copies:
            c.start()
        out_c.extend(copies)

    forward(0)
    for k in range(1, NCH):
        forward(k)
        relay(k - 1)
        if k == 1:
            for c in weights_in:
                c.wait()
        if k >= 3 and k % 2 == 1:
            p = (k - 3) // 2
            compute(p)
            if p >= 1:
                stage2(p - 1)
            if p >= 2:
                stage3(p - 2)
    relay(NCH - 1)
    compute(3)
    stage2(2)
    stage3(1)
    weight_grads(0)
    stage2(3)
    stage3(2)
    weight_grads(1)
    stage3(3)
    weight_grads(2)
    weight_grads(3)
    for q in range(DP):
        merge(q)

    own_back = pltpu.make_async_copy(rt_snd.at[0], rt_rcv.at[0], loc_sem.at[1])
    own_back.wait()
    for p in range(NPAIR):
        chunk_wait(rt_rcv, p, b_rcv, 16)
    copies = (
        pltpu.make_async_copy(rt_rcv, ret_ref, loc_sem.at[2]),
        pltpu.make_async_copy(sel, sel_ref, loc_sem.at[3]),
    )
    for c in copies:
        c.start()
    for k in range(NCH):
        chunk_wait(msg, k, a_snd)
        for c in (to_up[k], to_dn[k], rel_up[k], rel_dn[k]):
            c.wait_send()
    for p in range(NPAIR):
        chunk_wait(rt_snd, p, b_snd, 16)
        for c in rs_c[p] + fin_c[p]:
            c.wait_send()
    for c in pair_c:
        c.wait_send()
    for c in out_c:
        c.wait()
    for c in copies:
        c.wait()


def on_device(tokens, grad_out, routes, gates, replicated, w_gate, w_up, w_down):
    vmem = pl.BlockSpec(memory_space=pltpu.VMEM)
    hbm = pl.BlockSpec(memory_space=pl.ANY)
    dma = pltpu.SemaphoreType.DMA
    n_rows = SLOTS * CAP
    ret, sel, grad_gate, grad_up, grad_down = pl.pallas_call(
        kernel,
        out_shape=(
            jax.ShapeDtypeStruct((SLOTS, 16, RET), BF),
            jax.ShapeDtypeStruct((n_rows, TOK), BF),
            jax.ShapeDtypeStruct((1, D, HQ), BF),
            jax.ShapeDtypeStruct((1, D, HQ), BF),
            jax.ShapeDtypeStruct((1, HQ, D), BF),
        ),
        in_specs=[vmem] * 5 + [hbm] * 3,
        out_specs=(hbm,) * 5,
        scratch_shapes=[
            pltpu.VMEM((D, 2 * HQ), BF),
            pltpu.VMEM((HQ, D), BF),
            pltpu.VMEM((n_rows, TOK), BF),
            pltpu.VMEM((SLOTS, 16, MSG), BF),
            pltpu.VMEM((SLOTS, 16, MSG), BF),
            pltpu.VMEM((NCH, DP, 128, FQ), BF),
            pltpu.VMEM((n_rows, 128), F32),
            pltpu.VMEM((n_rows, 2 * HQ), BF),
            pltpu.VMEM((n_rows, HQ), BF),
            pltpu.VMEM((NPAIR, 128, FQ), BF),
            pltpu.VMEM((NPAIR, 64, FQ), BF),
            pltpu.VMEM((NPAIR, 64, FQ), BF),
            pltpu.VMEM((NPAIR, 128, FQ), F32),
            pltpu.VMEM((NPAIR, 128, FQ), F32),
            pltpu.VMEM((NPAIR, 128, FQ), F32),
            pltpu.VMEM((NPAIR, 2, 128, FQ), BF),
            pltpu.VMEM((NPAIR, 2, 128, FQ), BF),
            pltpu.VMEM((SLOTS, 16, RET), BF),
            pltpu.VMEM((SLOTS, 16, RET), BF),
            pltpu.VMEM((D, 2 * HQ), BF),
            pltpu.VMEM((DP, HQ, FQ), BF),
            pltpu.VMEM((D, 2 * HQ), BF),
            pltpu.VMEM((DP, HQ, FQ), BF),
            dma((3,)), dma((4,)),
            dma((NCH,)), dma((NCH,)),
            dma((NCH, 2)), dma((NCH, 2)),
            dma((NCH, 2)), dma((NCH, 2)),
            dma((NPAIR, 2)), dma((NPAIR, 2)),
            dma((NPAIR, 2)), dma((NPAIR, 2)),
            dma((NPAIR,)), dma((NPAIR,)),
            dma((DP, 2)), dma((DP, 2)),
            dma((DP, 3)),
        ],
        compiler_params=pltpu.CompilerParams(
            collective_id=0, has_side_effects=True, vmem_limit_bytes=60 * 2**20
        ),
        cost_estimate=pl.CostEstimate(flops=8 * 10**9, bytes_accessed=12 * 10**6, transcendentals=0),
    )(
        tokens, grad_out, routes.T, gates.astype(F32).T, replicated.reshape(1, 1),
        w_gate, w_up, w_down,
    )
    picks = sel.reshape(SLOTS, CAP, TOK)
    back = ret.reshape(SLOTS, 2, CAP, RET)
    grad_tokens = jnp.einsum("sjt,shjf->thf", picks, back, preferred_element_type=F32)
    grad_tokens = grad_tokens.reshape(TOK, 2 * RET)[:, :FQ].astype(BF)
    return grad_tokens, grad_gate, grad_up, grad_down


def solution(mesh):
    return jax.shard_map(
        on_device,
        mesh=mesh,
        in_specs=(
            P("expert", "dp"),
            P("expert", "dp"),
            P("expert", None),
            P("expert", None),
            P("expert"),
            P("expert", None, "dp"),
            P("expert", None, "dp"),
            P("expert", "dp", None),
        ),
        out_specs=(
            P("expert", "dp"),
            P("expert", None, "dp"),
            P("expert", None, "dp"),
            P("expert", "dp", None),
        ),
        check_vma=False,
    )
```

```python
import functools

import jax
import jax.numpy as jnp
from jax import lax
from jax.experimental import pallas as pl
from jax.experimental.pallas import tpu as pltpu
from jax.sharding import PartitionSpec as P

MESH = pl.DeviceIdType.MESH
BF, F32 = jnp.bfloat16, jnp.float32
D, H, DP = 3584, 1024, 4
FQ, HQ = D // DP, H // DP
TOK, CAP, SLOTS = 128, 8, 64
NX, NZ = 4, 8
VLIM = 50 * 2**20
NCH = 8
NPAIR = 4
NEAR = 3
FAR = NCH - NEAR
MSG = FQ + 128
FULL = D + 128
RET = 512


LANES = [(dx, dc) for dx in range(NX) for dc in (0, 1)]
FAR_Z = (2, -2, 3, -3, 4)
NEAR_Z = ((1, -1), (-1, 1), (0, 0))
OFFSETS = [(dx, FAR_Z[(k + m) % 5] % NZ, dc) for k in range(FAR) for m, (dx, dc) in enumerate(LANES)]
OFFSETS += [(dx, dz[m % 2] % NZ, dc) for dz in NEAR_Z for m, (dx, dc) in enumerate(LANES)]
OWN = OFFSETS.index((0, 0, 0))
BACK = [OFFSETS.index(((-dx) % NX, (-dz) % NZ, dc)) for dx, dz, dc in OFFSETS]


def dot(a, b, dims):
    return lax.dot_general(a, b, ((dims[0], dims[1]), ((), ())), preferred_element_type=F32)


NN, NT, TN = ((1,), (0,)), ((1,), (1,)), ((0,), (0,))


def kernel(
    tok_ref, dy_ref, routes_ref, gates_ref, flag_ref, wg_ref, wu_ref, wd_ref,
    rt_rcv, sel, gu_sum, gd_sum,
    wgu, wdn, full, msg, land, near_msg, near_land, rows, gcol, dgu, sh,
    rs_snd, rs_a, rs_b, p_up, p_dn, p_own, fin_snd, fin_rcv, rt_snd,
    gu_mine, gd_mine, gu_theirs, gd_theirs,
    w_sem, loc_sem, a_snd, a_rcv, y_snd, y_rcv, r_snd, r_rcv, q_snd, q_rcv, f_snd, f_rcv,
    b_snd, b_rcv, g_snd, g_rcv, t_snd, t_rcv, u_snd, u_rcv,
):
    d = lax.axis_index("dp")
    e = lax.axis_index("expert")
    x0, z0, c0 = e // 16, (e // 2) % NZ, e % 2
    up, dn, op = (d + 1) % DP, (d + 3) % DP, (d + 2) % DP

    def peer(o):
        dx, dz, dc = OFFSETS[o]
        return ((x0 + dx) % NX * NZ + (z0 + dz) % NZ) * 2 + (c0 + dc) % 2

    def remote(src, dst, s, r, dev):
        return pltpu.make_async_remote_copy(src, dst, s, r, device_id=dev, device_id_type=MESH)

    weights_in = [
        pltpu.make_async_copy(wg_ref.at[0], wgu.at[:, pl.ds(0, HQ)], w_sem.at[0]),
        pltpu.make_async_copy(wu_ref.at[0], wgu.at[:, pl.ds(HQ, HQ)], w_sem.at[1]),
        pltpu.make_async_copy(wd_ref.at[0], wdn, w_sem.at[2]),
    ]
    for c in weights_in:
        c.start()

    barrier = pltpu.get_barrier_semaphore()
    for o in range(SLOTS):
        if o == OWN:
            continue
        pl.semaphore_signal(barrier, inc=1, device_id=(d, peer(o)), device_id_type=MESH)
    for q in range(1, DP):
        pl.semaphore_signal(barrier, inc=1, device_id=((d + q) % DP, e), device_id_type=MESH)

    io = lax.broadcasted_iota(jnp.int32, (SLOTS, TOK), 0)
    slot = jnp.zeros((SLOTS, TOK), jnp.int32)
    for o in range(SLOTS):
        slot = jnp.where(io == o, peer(o), slot)
    on0 = routes_ref[0:1, :] == slot
    on1 = routes_ref[1:2, :] == slot
    hot0 = on0.astype(F32)
    hot1 = on1.astype(F32)
    before = (
        lax.broadcasted_iota(jnp.int32, (TOK, TOK), 0) < lax.broadcasted_iota(jnp.int32, (TOK, TOK), 1)
    ).astype(BF)
    rank0 = dot(hot0.astype(BF), before, NN)
    rank1 = dot(hot1.astype(BF), before, NN) + jnp.sum(hot0, axis=1, keepdims=True)
    rank0 = jnp.where(on0, rank0, -1.0).astype(BF)
    rank1 = jnp.where(on1, rank1, -1.0).astype(BF)
    n_rows = SLOTS * CAP
    ui = lax.broadcasted_iota(jnp.int32, (n_rows, SLOTS), 0)
    spread = ((ui >> 3) == lax.broadcasted_iota(jnp.int32, (n_rows, SLOTS), 1)).astype(BF)
    place = (lax.broadcasted_iota(jnp.int32, (n_rows, TOK), 0) & 7).astype(F32)
    sel0 = (dot(spread, rank0, NN) == place).astype(F32)
    sel1 = (dot(spread, rank1, NN) == place).astype(F32)
    sel[...] = (sel0 + sel1).astype(BF)
    gates = gates_ref[...].astype(F32)
    gate_of = (sel0 * gates[0:1, :] + sel1 * gates[1:2, :]).astype(BF)
    gcol[...] = dot(gate_of, jnp.ones((TOK, 128), BF), NN)

    pl.semaphore_wait(barrier, SLOTS - 1 + DP - 1)

    src_up = [
        remote(tok_ref, full.at[d, 0], t_snd.at[0], t_rcv.at[0], (up, e)),
        remote(dy_ref, full.at[d, 1], t_snd.at[1], t_rcv.at[1], (up, e)),
    ]
    src_dn = [
        remote(dy_ref, full.at[d, 1], t_snd.at[2], t_rcv.at[2], (dn, e)),
        remote(tok_ref, full.at[d, 0], t_snd.at[3], t_rcv.at[3], (dn, e)),
    ]
    for i in range(2):
        src_up[i].start()
        src_dn[i].start()

    def pack(k, out, at, lane, xs, ys):
        s = sel[k * 64:(k + 1) * 64, :]
        xk = dot(s, xs, NN).reshape(8, 8, FQ)
        yk = dot(s, ys, NN).reshape(8, 8, FQ)
        lanes = pl.ds(lane, FQ) if isinstance(lane, int) else pl.ds(pl.multiple_of(lane, 128), FQ)
        out[at:at + 8, :, lanes] = jnp.concatenate([xk, yk], axis=1).astype(BF)

    def pack_gates(k, out, at, lane):
        gk = gcol[k * 64:(k + 1) * 64, :].reshape(8, 8, 128)
        out[at:at + 8, :, lane:lane + 128] = jnp.concatenate([gk, gk], axis=1).astype(BF)

    def send(k, src, dst, base):
        for o in range(8 * k, 8 * k + 8):
            if o == OWN:
                pltpu.make_async_copy(src.at[o - base], dst.at[o - base], loc_sem.at[0]).start()
                continue
            remote(src.at[o - base], dst.at[o - base], a_snd.at[k], a_rcv.at[k], (d, peer(o))).start()

    for k in range(FAR):
        pack(k, msg, 8 * k, 0, tok_ref[...], dy_ref[...])
        pack_gates(k, msg, 8 * k, FQ)
        send(k, msg, land, 0)

    def relay_source():
        src_up[0].wait_recv()
        part = full.at[dn, 0]
        src_up.append(remote(part, part, u_snd.at[0], u_rcv.at[0], (up, e)))
        src_up[2].start()
        src_dn[0].wait_recv()
        part = full.at[up, 1]
        src_dn.append(remote(part, part, u_snd.at[1], u_rcv.at[1], (dn, e)))
        src_dn[2].start()

    def send_near():
        for c in (src_up[1], src_dn[1], src_up[2], src_dn[2]):
            c.wait_recv()
        full[d, 0] = tok_ref[...]
        full[d, 1] = dy_ref[...]
        for k in range(FAR, NCH):
            at = 8 * (k - FAR)
            for q in range(DP):
                pack(k, near_msg, at, q * FQ, full[q, 0], full[q, 1])
            pack_gates(k, near_msg, at, D)
            send(k, near_msg, near_land, 8 * FAR)

    def chunk_wait(buf, k, sem, per=8, base=0):
        lo, n = per * k, per
        if lo <= OWN < lo + per:
            n = per - 1
        block = buf.at[pl.ds(lo - base, n)]
        pltpu.make_async_copy(block, block, sem.at[k]).wait()

    to_up, to_dn, rel_up, rel_dn = {}, {}, {}, {}

    def unpack(k, block, lane, q):
        rows[k, q, 0:64, :] = block[:, 0:8, lane:lane + FQ].reshape(64, FQ).astype(BF)
        rows[k, q, 64:128, :] = block[:, 8:16, lane:lane + FQ].reshape(64, FQ).astype(BF)

    def forward(k):
        chunk_wait(land, k, a_rcv)
        block = land[k * 8:(k + 1) * 8].astype(F32)
        unpack(k, block, 0, d)
        gcol[k * 64:(k + 1) * 64, :] = block[:, 0:8, FQ:MSG].reshape(64, 128)
        mine = rows.at[k, d]
        to_up[k] = remote(mine, mine, y_snd.at[k, 0], y_rcv.at[k, 0], (up, e))
        to_dn[k] = remote(mine, mine, y_snd.at[k, 1], y_rcv.at[k, 1], (dn, e))
        to_up[k].start()
        to_dn[k].start()

    def take_near(k):
        if 8 * k <= OWN < 8 * k + 8:
            at = OWN - 8 * FAR
            pltpu.make_async_copy(near_msg.at[at], near_land.at[at], loc_sem.at[0]).wait()
        chunk_wait(near_land, k, a_rcv, 8, 8 * FAR)
        at = 8 * (k - FAR)
        for q in range(DP):
            block = near_land[at:at + 8, :, q * FQ:(q + 1) * FQ].astype(F32)
            unpack(k, block, 0, q)
        block = near_land[at:at + 8, :, D:FULL].astype(F32)
        gcol[k * 64:(k + 1) * 64, :] = block[:, 0:8, :].reshape(64, 128)

    def relay(k):
        to_up[k].wait_recv()
        part = rows.at[k, dn, pl.ds(0, 64)]
        rel_up[k] = remote(part, part, r_snd.at[k, 0], r_rcv.at[k, 0], (up, e))
        rel_up[k].start()
        to_dn[k].wait_recv()
        part = rows.at[k, up, pl.ds(64, 64)]
        rel_dn[k] = remote(part, part, r_snd.at[k, 1], r_rcv.at[k, 1], (dn, e))
        rel_dn[k].start()

    def row_part(p, q):
        rng = pl.ds(pl.multiple_of(q * FQ, FQ), FQ)
        return dot(dgu[p * 128:(p + 1) * 128, :], wgu[rng, :], NT)

    rs_c = {}

    def compute(p):
        for k in (2 * p, 2 * p + 1):
            if k < FAR:
                rel_up[k].wait_recv()
                rel_dn[k].wait_recv()
            else:
                take_near(k)
        pre = jnp.zeros((128, 2 * HQ), F32)
        dh = jnp.zeros((128, HQ), F32)
        for q in range(DP):
            xq = rows[2 * p:2 * p + 2, q, 0:64, :].reshape(128, FQ)
            yq = rows[2 * p:2 * p + 2, q, 64:128, :].reshape(128, FQ)
            pre = pre + dot(xq, wgu[q * FQ:(q + 1) * FQ, :], NN)
            dh = dh + dot(yq, wdn[:, q * FQ:(q + 1) * FQ], NT)
        g = gcol[p * 128:(p + 1) * 128, :]
        g = jnp.concatenate([g, g], axis=1)
        pg, pu = pre[:, 0:HQ], pre[:, HQ:]
        sig = jax.nn.sigmoid(pg)
        act = pg * sig
        dh = g * dh
        span = slice(p * 128, (p + 1) * 128)
        sh[span, :] = (g * act * pu).astype(BF)
        dgu[span, 0:HQ] = (dh * pu * sig * (1.0 + pg * (1.0 - sig))).astype(BF)
        dgu[span, HQ:] = (dh * act).astype(BF)
        rs_snd[p] = row_part(p, op).astype(BF)
        rs_c[p] = (
            remote(rs_snd.at[p, pl.ds(0, 64)], rs_a.at[p], q_snd.at[p, 0], q_rcv.at[p, 0], (up, e)),
            remote(rs_snd.at[p, pl.ds(64, 64)], rs_b.at[p], q_snd.at[p, 1], q_rcv.at[p, 1], (dn, e)),
        )
        for c in rs_c[p]:
            c.start()
        p_up[p] = row_part(p, up)
        p_dn[p] = row_part(p, dn)
        p_own[p] = row_part(p, d)

    fin_c = {}

    def stage2(p):
        rs_c[p][0].wait_recv()
        fin_snd[p, 0, 0:64, :] = (p_up[p, 0:64, :] + rs_a[p].astype(F32)).astype(BF)
        fin_snd[p, 0, 64:128, :] = p_up[p, 64:128, :].astype(BF)
        first = remote(fin_snd.at[p, 0], fin_rcv.at[p, 0], f_snd.at[p, 0], f_rcv.at[p, 0], (up, e))
        first.start()
        rs_c[p][1].wait_recv()
        fin_snd[p, 1, 0:64, :] = p_dn[p, 0:64, :].astype(BF)
        fin_snd[p, 1, 64:128, :] = (p_dn[p, 64:128, :] + rs_b[p].astype(F32)).astype(BF)
        second = remote(fin_snd.at[p, 1], fin_rcv.at[p, 1], f_snd.at[p, 1], f_rcv.at[p, 1], (dn, e))
        second.start()
        fin_c[p] = (first, second)

    def stage3(p):
        fin_c[p][0].wait_recv()
        fin_c[p][1].wait_recv()
        total = p_own[p] + fin_rcv[p, 0].astype(F32) + fin_rcv[p, 1].astype(F32)
        total = total.reshape(16, 8, FQ)
        tail = jnp.concatenate([total[:, :, RET:FQ], jnp.zeros((16, 8, 2 * RET - FQ), F32)], axis=2)
        rt_snd[16 * p:16 * p + 16] = jnp.concatenate([total[:, :, 0:RET], tail], axis=1).astype(BF)
        for o in range(16 * p, 16 * p + 16):
            if o == OWN:
                pltpu.make_async_copy(rt_snd.at[o], rt_rcv.at[o], loc_sem.at[1]).start()
                continue
            remote(rt_snd.at[o], rt_rcv.at[o], b_snd.at[p], b_rcv.at[p], (d, peer(BACK[o]))).start()

    pair_c = []
    partner = (d, e + 1 - 2 * c0)

    def weight_grads(q):
        xq = rows[:, q, 0:64, :].reshape(n_rows, FQ)
        gu_mine[q * FQ:(q + 1) * FQ, :] = dot(xq, dgu[...], TN).astype(BF)
        part = pl.ds(q * FQ, FQ)
        c = remote(gu_mine.at[part], gu_theirs.at[part], g_snd.at[q, 0], g_rcv.at[q, 0], partner)
        c.start()
        pair_c.append(c)
        yq = rows[:, q, 64:128, :].reshape(n_rows, FQ)
        gd_mine[q] = dot(sh[...], yq, TN).astype(BF)
        c = remote(gd_mine.at[q], gd_theirs.at[q], g_snd.at[q, 1], g_rcv.at[q, 1], partner)
        c.start()
        pair_c.append(c)

    def merge(q):
        replica = flag_ref[...] == 1
        pair_c[2 * q].wait_recv()
        mine = gu_mine[q * FQ:(q + 1) * FQ, :].astype(F32)
        theirs = gu_theirs[q * FQ:(q + 1) * FQ, :].astype(F32)
        gu_sum[q * FQ:(q + 1) * FQ, :] = (mine + jnp.where(replica, theirs, 0.0)).astype(BF)
        pair_c[2 * q + 1].wait_recv()
        mine = gd_mine[q].astype(F32)
        theirs = gd_theirs[q].astype(F32)
        gd_sum[q] = (mine + jnp.where(replica, theirs, 0.0)).astype(BF)

    relay_source()
    forward(0)
    send_near()
    forward(1)
    relay(0)
    forward(2)
    relay(1)
    for c in weights_in:
        c.wait()
    forward(3)
    relay(2)
    compute(0)
    forward(4)
    relay(3)
    stage2(0)
    relay(4)
    compute(1)
    stage3(0)
    stage2(1)
    compute(2)
    stage3(1)
    stage2(2)
    compute(3)
    stage3(2)
    weight_grads(0)
    stage2(3)
    weight_grads(1)
    stage3(3)
    weight_grads(2)
    weight_grads(3)
    for q in range(DP):
        merge(q)

    pltpu.make_async_copy(rt_snd.at[OWN], rt_rcv.at[OWN], loc_sem.at[1]).wait()
    for p in range(NPAIR):
        chunk_wait(rt_rcv, p, b_rcv, 16)
    for k in range(FAR):
        chunk_wait(msg, k, a_snd)
        for c in (to_up[k], to_dn[k], rel_up[k], rel_dn[k]):
            c.wait_send()
    for k in range(FAR, NCH):
        chunk_wait(near_msg, k, a_snd, 8, 8 * FAR)
    for c in src_up + src_dn:
        c.wait_send()
    for p in range(NPAIR):
        chunk_wait(rt_snd, p, b_snd, 16)
        for c in rs_c[p] + fin_c[p]:
            c.wait_send()
    for c in pair_c:
        c.wait_send()


def finish(ret_ref, sel_ref, gu_ref, gd_ref, gt_ref, og_ref, ou_ref, od_ref, sem):
    copies = [
        pltpu.make_async_copy(gu_ref.at[:, pl.ds(0, HQ)], og_ref.at[0], sem.at[0]),
        pltpu.make_async_copy(gu_ref.at[:, pl.ds(HQ, HQ)], ou_ref.at[0], sem.at[1]),
    ]
    for q in range(DP):
        copies.append(pltpu.make_async_copy(gd_ref.at[q], od_ref.at[0, :, pl.ds(q * FQ, FQ)], sem.at[2 + q]))
    for c in copies:
        c.start()
    picks = sel_ref[...].astype(F32).reshape(SLOTS, CAP, TOK)
    none = jnp.zeros_like(picks)
    back = ret_ref[...].reshape(SLOTS * 16, RET)
    low = jnp.concatenate([picks, none], axis=1).reshape(SLOTS * 16, TOK).astype(BF)
    high = jnp.concatenate([none, picks], axis=1).reshape(SLOTS * 16, TOK).astype(BF)
    gt_ref[:, 0:RET] = dot(low, back, TN).astype(BF)
    gt_ref[:, RET:FQ] = dot(high, back, TN)[:, 0:FQ - RET].astype(BF)
    for c in copies:
        c.wait()


def on_device(tokens, grad_out, routes, gates, replicated, w_gate, w_up, w_down):
    vmem = pl.BlockSpec(memory_space=pltpu.VMEM)
    hbm = pl.BlockSpec(memory_space=pl.ANY)
    dma = pltpu.SemaphoreType.DMA
    n_rows = SLOTS * CAP
    results = pl.pallas_call(
        kernel,
        out_shape=(
            pltpu.VMEM((SLOTS, 16, RET), BF),
            pltpu.VMEM((n_rows, TOK), BF),
            pltpu.VMEM((D, 2 * HQ), BF),
            pltpu.VMEM((DP, HQ, FQ), BF),
        ),
        in_specs=[vmem] * 5 + [hbm] * 3,
        out_specs=(vmem,) * 4,
        scratch_shapes=[
            pltpu.VMEM((D, 2 * HQ), BF),
            pltpu.VMEM((HQ, D), BF),
            pltpu.VMEM((DP, 2, TOK, FQ), BF),
            pltpu.VMEM((8 * FAR, 16, MSG), BF),
            pltpu.VMEM((8 * FAR, 16, MSG), BF),
            pltpu.VMEM((8 * NEAR, 16, FULL), BF),
            pltpu.VMEM((8 * NEAR, 16, FULL), BF),
            pltpu.VMEM((NCH, DP, 128, FQ), BF),
            pltpu.VMEM((n_rows, 128), F32),
            pltpu.VMEM((n_rows, 2 * HQ), BF),
            pltpu.VMEM((n_rows, HQ), BF),
            pltpu.VMEM((NPAIR, 128, FQ), BF),
            pltpu.VMEM((NPAIR, 64, FQ), BF),
            pltpu.VMEM((NPAIR, 64, FQ), BF),
            pltpu.VMEM((NPAIR, 128, FQ), F32),
            pltpu.VMEM((NPAIR, 128, FQ), F32),
            pltpu.VMEM((NPAIR, 128, FQ), F32),
            pltpu.VMEM((NPAIR, 2, 128, FQ), BF),
            pltpu.VMEM((NPAIR, 2, 128, FQ), BF),
            pltpu.VMEM((SLOTS, 16, RET), BF),
            pltpu.VMEM((D, 2 * HQ), BF),
            pltpu.VMEM((DP, HQ, FQ), BF),
            pltpu.VMEM((D, 2 * HQ), BF),
            pltpu.VMEM((DP, HQ, FQ), BF),
            dma((3,)), dma((2,)),
            dma((NCH,)), dma((NCH,)),
            dma((NCH, 2)), dma((NCH, 2)),
            dma((NCH, 2)), dma((NCH, 2)),
            dma((NPAIR, 2)), dma((NPAIR, 2)),
            dma((NPAIR, 2)), dma((NPAIR, 2)),
            dma((NPAIR,)), dma((NPAIR,)),
            dma((DP, 2)), dma((DP, 2)),
            dma((4,)), dma((4,)), dma((2,)), dma((2,)),
        ],
        compiler_params=pltpu.CompilerParams(
            collective_id=0, has_side_effects=True, vmem_limit_bytes=VLIM
        ),
        cost_estimate=pl.CostEstimate(flops=8 * 10**9, bytes_accessed=12 * 10**6, transcendentals=0),
    )(
        tokens, grad_out, routes.T, gates.T, replicated.reshape(1, 1),
        w_gate, w_up, w_down,
    )
    return pl.pallas_call(
        finish,
        out_shape=(
            jax.ShapeDtypeStruct((TOK, FQ), BF),
            jax.ShapeDtypeStruct((1, D, HQ), BF),
            jax.ShapeDtypeStruct((1, D, HQ), BF),
            jax.ShapeDtypeStruct((1, HQ, D), BF),
        ),
        in_specs=[vmem] * 4,
        out_specs=(vmem,) + (hbm,) * 3,
        scratch_shapes=[dma((2 + DP,))],
        compiler_params=pltpu.CompilerParams(vmem_limit_bytes=16 * 2**20),
        cost_estimate=pl.CostEstimate(flops=3 * 10**8, bytes_accessed=7 * 10**6, transcendentals=0),
    )(*results)


def solution(mesh):
    return jax.shard_map(
        on_device,
        mesh=mesh,
        in_specs=(
            P("expert", "dp"),
            P("expert", "dp"),
            P("expert", None),
            P("expert", None),
            P("expert"),
            P("expert", None, "dp"),
            P("expert", None, "dp"),
            P("expert", "dp", None),
        ),
        out_specs=(
            P("expert", "dp"),
            P("expert", None, "dp"),
            P("expert", None, "dp"),
            P("expert", "dp", None),
        ),
        check_vma=False,
    )
```

```python
import functools

import jax
import jax.numpy as jnp
from jax import lax
from jax.experimental import pallas as pl
from jax.experimental.pallas import tpu as pltpu
from jax.sharding import PartitionSpec as P

MESH = pl.DeviceIdType.MESH
BF, F32 = jnp.bfloat16, jnp.float32
D, H, DP = 3584, 1024, 4
FQ, HQ = D // DP, H // DP
TOK, CAP, SLOTS = 128, 8, 64
NX, NZ = 4, 8
VLIM = 50 * 2**20
NCH = 8
NPAIR = 4
NEAR = 3
FAR = NCH - NEAR
RET = 512


NEAR_OFFSETS = [(dx, dz, dc) for dx, dz in ((0, 2), (0, -2), (1, 1), (-1, -1)) for dc in (0, 1)]
NEAR_OFFSETS += [(dx, dz, dc) for dx, dz in ((0, 1), (0, -1), (1, -1), (-1, 1)) for dc in (0, 1)]
NEAR_OFFSETS += [(dx, 0, dc) for dx in (0, 1, -1, 2) for dc in (0, 1)]
NEAR_OFFSETS = [(dx % NX, dz % NZ, dc) for dx, dz, dc in NEAR_OFFSETS]
FAR_OFFSETS = [(dx, dz, dc) for dz in range(NZ) for dx in range(NX) for dc in (0, 1)]
FAR_OFFSETS = [o for o in FAR_OFFSETS if o not in NEAR_OFFSETS]
OFFSETS = [o for k in range(FAR) for o in FAR_OFFSETS[k::FAR]] + NEAR_OFFSETS
OWN = OFFSETS.index((0, 0, 0))
BACK = [OFFSETS.index(((-dx) % NX, (-dz) % NZ, dc)) for dx, dz, dc in OFFSETS]


def dot(a, b, dims):
    return lax.dot_general(a, b, ((dims[0], dims[1]), ((), ())), preferred_element_type=F32)


NN, NT, TN = ((1,), (0,)), ((1,), (1,)), ((0,), (0,))


def kernel(
    tok_ref, dy_ref, routes_ref, gates_ref, flag_ref, wg_ref, wu_ref, wd_ref,
    rt_rcv, sel, gu_sum, gd_sum,
    wgu, wdn, full, msg, land, near_msg, near_land, rows, g_msg, g_land, g_rows, dgu, sh,
    rs_snd, rs_a, rs_b, p_up, p_dn, p_own, fin_snd, fin_rcv, rt_snd,
    gu_mine, gd_mine, gu_theirs, gd_theirs,
    w_sem, loc_sem, a_snd, a_rcv, y_snd, y_rcv, r_snd, r_rcv, q_snd, q_rcv, f_snd, f_rcv,
    b_snd, b_rcv, g_snd, g_rcv, t_snd, t_rcv, u_snd, u_rcv, gt_snd, gt_rcv, gs_snd, gs_rcv, sync,
):
    d = lax.axis_index("dp")
    e = lax.axis_index("expert")
    x0, z0, c0 = e // 16, (e // 2) % NZ, e % 2
    up, dn, op = (d + 1) % DP, (d + 3) % DP, (d + 2) % DP

    def peer(o):
        dx, dz, dc = OFFSETS[o]
        return ((x0 + dx) % NX * NZ + (z0 + dz) % NZ) * 2 + (c0 + dc) % 2

    def remote(src, dst, s, r, dev):
        return pltpu.make_async_remote_copy(src, dst, s, r, device_id=dev, device_id_type=MESH)

    weights_in = [
        pltpu.make_async_copy(wg_ref.at[0], wgu.at[:, pl.ds(0, HQ)], w_sem.at[0]),
        pltpu.make_async_copy(wu_ref.at[0], wgu.at[:, pl.ds(HQ, HQ)], w_sem.at[1]),
        pltpu.make_async_copy(wd_ref.at[0], wdn, w_sem.at[2]),
    ]
    for c in weights_in:
        c.start()

    barrier = pltpu.get_barrier_semaphore()
    def greet(sem, devices):
        for dev in devices:
            pl.semaphore_signal(sem, inc=1, device_id=dev, device_id_type=MESH)

    along_x = [(d, ((x0 + i) % NX * NZ + z0) * 2 + c0) for i in range(1, NX)]
    along_z = [(d, (x0 * NZ + (z0 + i) % NZ) * 2 + c0) for i in range(1, NZ)]
    partner = (d, e + 1 - 2 * c0)
    along_y = [((d + i) % DP, e) for i in range(1, DP)]
    greet(barrier, along_y + along_z + along_x + [partner])

    io = lax.broadcasted_iota(jnp.int32, (SLOTS, TOK), 0)
    slot = jnp.zeros((SLOTS, TOK), jnp.int32)
    for o in range(SLOTS):
        slot = jnp.where(io == o, peer(o), slot)
    on0 = routes_ref[0:1, :] == slot
    on1 = routes_ref[1:2, :] == slot
    hot0 = on0.astype(F32)
    hot1 = on1.astype(F32)
    before = (
        lax.broadcasted_iota(jnp.int32, (TOK, TOK), 0) < lax.broadcasted_iota(jnp.int32, (TOK, TOK), 1)
    ).astype(BF)
    rank0 = dot(hot0.astype(BF), before, NN)
    rank1 = dot(hot1.astype(BF), before, NN) + jnp.sum(hot0, axis=1, keepdims=True)
    rank0 = jnp.where(on0, rank0, -1.0).astype(BF)
    rank1 = jnp.where(on1, rank1, -1.0).astype(BF)
    n_rows = SLOTS * CAP
    ui = lax.broadcasted_iota(jnp.int32, (n_rows, SLOTS), 0)
    spread = ((ui >> 3) == lax.broadcasted_iota(jnp.int32, (n_rows, SLOTS), 1)).astype(BF)
    place = (lax.broadcasted_iota(jnp.int32, (n_rows, TOK), 0) & 7).astype(F32)
    sel0 = (dot(spread, rank0, NN) == place).astype(F32)
    sel1 = (dot(spread, rank1, NN) == place).astype(F32)
    sel[...] = (sel0 + sel1).astype(BF)
    gates = gates_ref[...].astype(F32)
    gate_of = (sel0 * gates[0:1, :] + sel1 * gates[1:2, :]).astype(BF)
    gates_of = dot(gate_of, jnp.ones((TOK, 128), BF), NN).reshape(SLOTS, CAP, 128)
    g_msg[...] = jnp.concatenate([gates_of, gates_of], axis=1).astype(BF)

    pl.semaphore_wait(barrier, DP + NZ + NX - 3 + 1)
    greet(sync.at[0], along_x)

    src_up = [
        remote(tok_ref, full.at[d, 0], t_snd.at[0], t_rcv.at[0], (up, e)),
        remote(dy_ref, full.at[d, 1], t_snd.at[1], t_rcv.at[1], (up, e)),
    ]
    src_dn = [
        remote(dy_ref, full.at[d, 1], t_snd.at[2], t_rcv.at[2], (dn, e)),
        remote(tok_ref, full.at[d, 0], t_snd.at[3], t_rcv.at[3], (dn, e)),
    ]
    for i in range(2):
        src_up[i].start()
        src_dn[i].start()

    def pack(k, out, at, lane, xs, ys):
        s = sel[k * 64:(k + 1) * 64, :]
        xk = dot(s, xs, NN).reshape(8, 8, FQ)
        yk = dot(s, ys, NN).reshape(8, 8, FQ)
        lanes = pl.ds(lane, FQ) if isinstance(lane, int) else pl.ds(pl.multiple_of(lane, 128), FQ)
        out[at:at + 8, :, lanes] = jnp.concatenate([xk, yk], axis=1).astype(BF)

    def send(k, src, dst, base):
        for o in range(8 * k, 8 * k + 8):
            if o == OWN:
                pltpu.make_async_copy(src.at[o - base], dst.at[o - base], loc_sem.at[0]).start()
                continue
            remote(src.at[o - base], dst.at[o - base], a_snd.at[k], a_rcv.at[k], (d, peer(o))).start()

    def each_dp(act):
        for p in range(DP):
            pl.when(d == p)(functools.partial(act, p))

    def send_gates(p):
        for o in range(16 * p, 16 * p + 16):
            if o == OWN:
                pltpu.make_async_copy(g_msg.at[o], g_land.at[o - 16 * p], loc_sem.at[2]).start()
                continue
            remote(g_msg.at[o], g_land.at[o - 16 * p], gt_snd.at[0], gt_rcv.at[0], (d, peer(o))).start()

    def gates_wait(sem, p):
        n = 15 if 16 * p <= OWN < 16 * p + 16 else 16
        block = g_land.at[pl.ds(0, n)]
        pltpu.make_async_copy(block, block, sem.at[0]).wait()

    def take_gates(p):
        if 16 * p <= OWN < 16 * p + 16:
            pltpu.make_async_copy(g_msg.at[OWN], g_land.at[OWN - 16 * p], loc_sem.at[2]).wait()
        gates_wait(gt_rcv, p)

    def share_gates():
        each_dp(take_gates)
        g_rows[d] = g_land[...].astype(F32)[:, 0:8, :].reshape(128, 128).astype(BF)
        for i, to in enumerate((up, op, dn)):
            gate_c.append(remote(g_rows.at[d], g_rows.at[d], gs_snd.at[i], gs_rcv.at[i], (to, e)))
            gate_c[i].start()

    gate_c = []
    for k in range(FAR):
        pack(k, msg, 8 * k, 0, tok_ref[...], dy_ref[...])
        if k == 0:
            pl.semaphore_wait(sync.at[0], NX - 1)
            greet(sync.at[1], [partner])
            pl.semaphore_wait(sync.at[1], 1)
            each_dp(send_gates)
        send(k, msg, land, 0)

    def relay_source():
        src_up[0].wait_recv()
        part = full.at[dn, 0]
        src_up.append(remote(part, part, u_snd.at[0], u_rcv.at[0], (up, e)))
        src_up[2].start()
        src_dn[0].wait_recv()
        part = full.at[up, 1]
        src_dn.append(remote(part, part, u_snd.at[1], u_rcv.at[1], (dn, e)))
        src_dn[2].start()

    def send_near():
        for c in (src_up[1], src_dn[1], src_up[2], src_dn[2]):
            c.wait_recv()
        full[d, 0] = tok_ref[...]
        full[d, 1] = dy_ref[...]
        for k in range(FAR, NCH):
            at = 8 * (k - FAR)
            for q in range(DP):
                pack(k, near_msg, at, q * FQ, full[q, 0], full[q, 1])
            send(k, near_msg, near_land, 8 * FAR)

    def chunk_wait(buf, k, sem, per=8, base=0):
        lo, n = per * k, per
        if lo <= OWN < lo + per:
            n = per - 1
        block = buf.at[pl.ds(lo - base, n)]
        pltpu.make_async_copy(block, block, sem.at[k]).wait()

    to_up, to_dn, rel_up, rel_dn = {}, {}, {}, {}

    def unpack(k, block, lane, q):
        rows[k, q, 0:64, :] = block[:, 0:8, lane:lane + FQ].reshape(64, FQ).astype(BF)
        rows[k, q, 64:128, :] = block[:, 8:16, lane:lane + FQ].reshape(64, FQ).astype(BF)

    def forward(k):
        chunk_wait(land, k, a_rcv)
        block = land[k * 8:(k + 1) * 8].astype(F32)
        unpack(k, block, 0, d)
        mine = rows.at[k, d]
        to_up[k] = remote(mine, mine, y_snd.at[k, 0], y_rcv.at[k, 0], (up, e))
        to_dn[k] = remote(mine, mine, y_snd.at[k, 1], y_rcv.at[k, 1], (dn, e))
        to_up[k].start()
        to_dn[k].start()

    def take_near(k):
        if 8 * k <= OWN < 8 * k + 8:
            at = OWN - 8 * FAR
            pltpu.make_async_copy(near_msg.at[at], near_land.at[at], loc_sem.at[0]).wait()
        chunk_wait(near_land, k, a_rcv, 8, 8 * FAR)
        at = 8 * (k - FAR)
        for q in range(DP):
            block = near_land[at:at + 8, :, q * FQ:(q + 1) * FQ].astype(F32)
            unpack(k, block, 0, q)

    def relay(k):
        to_up[k].wait_recv()
        part = rows.at[k, dn, pl.ds(0, 64)]
        rel_up[k] = remote(part, part, r_snd.at[k, 0], r_rcv.at[k, 0], (up, e))
        rel_up[k].start()
        to_dn[k].wait_recv()
        part = rows.at[k, up, pl.ds(64, 64)]
        rel_dn[k] = remote(part, part, r_snd.at[k, 1], r_rcv.at[k, 1], (dn, e))
        rel_dn[k].start()

    def row_part(p, q):
        rng = pl.ds(pl.multiple_of(q * FQ, FQ), FQ)
        return dot(dgu[p * 128:(p + 1) * 128, :], wgu[rng, :], NT)

    rs_c = {}

    def compute(p):
        for k in (2 * p, 2 * p + 1):
            if k < FAR:
                rel_up[k].wait_recv()
                rel_dn[k].wait_recv()
            else:
                take_near(k)
        pre = jnp.zeros((128, 2 * HQ), F32)
        dh = jnp.zeros((128, HQ), F32)
        for q in range(DP):
            xq = rows[2 * p:2 * p + 2, q, 0:64, :].reshape(128, FQ)
            yq = rows[2 * p:2 * p + 2, q, 64:128, :].reshape(128, FQ)
            pre = pre + dot(xq, wgu[q * FQ:(q + 1) * FQ, :], NN)
            dh = dh + dot(yq, wdn[:, q * FQ:(q + 1) * FQ], NT)
        g = g_rows[p].astype(F32)
        g = jnp.concatenate([g, g], axis=1)
        pg, pu = pre[:, 0:HQ], pre[:, HQ:]
        sig = jax.nn.sigmoid(pg)
        act = pg * sig
        dh = g * dh
        span = slice(p * 128, (p + 1) * 128)
        sh[span, :] = (g * act * pu).astype(BF)
        dgu[span, 0:HQ] = (dh * pu * sig * (1.0 + pg * (1.0 - sig))).astype(BF)
        dgu[span, HQ:] = (dh * act).astype(BF)
        rs_snd[2 * p:2 * p + 2] = row_part(p, op).astype(BF).reshape(2, 64, FQ)
        for k in (2 * p, 2 * p + 1):
            rs_c[k] = (
                remote(rs_snd.at[k, pl.ds(0, 32)], rs_a.at[k], q_snd.at[k, 0], q_rcv.at[k, 0], (up, e)),
                remote(rs_snd.at[k, pl.ds(32, 32)], rs_b.at[k], q_snd.at[k, 1], q_rcv.at[k, 1], (dn, e)),
            )
            for c in rs_c[k]:
                c.start()
        p_up[2 * p:2 * p + 2] = row_part(p, up).reshape(2, 64, FQ)
        p_dn[2 * p:2 * p + 2] = row_part(p, dn).reshape(2, 64, FQ)
        p_own[2 * p:2 * p + 2] = row_part(p, d).reshape(2, 64, FQ)

    fin_c = {}

    def stage2(k):
        rs_c[k][0].wait_recv()
        fin_snd[k, 0, 0:32, :] = (p_up[k, 0:32, :] + rs_a[k].astype(F32)).astype(BF)
        fin_snd[k, 0, 32:64, :] = p_up[k, 32:64, :].astype(BF)
        first = remote(fin_snd.at[k, 0], fin_rcv.at[k, 0], f_snd.at[k, 0], f_rcv.at[k, 0], (up, e))
        first.start()
        rs_c[k][1].wait_recv()
        fin_snd[k, 1, 0:32, :] = p_dn[k, 0:32, :].astype(BF)
        fin_snd[k, 1, 32:64, :] = (p_dn[k, 32:64, :] + rs_b[k].astype(F32)).astype(BF)
        second = remote(fin_snd.at[k, 1], fin_rcv.at[k, 1], f_snd.at[k, 1], f_rcv.at[k, 1], (dn, e))
        second.start()
        fin_c[k] = (first, second)

    def stage3(k):
        fin_c[k][0].wait_recv()
        fin_c[k][1].wait_recv()
        total = p_own[k] + fin_rcv[k, 0].astype(F32) + fin_rcv[k, 1].astype(F32)
        total = total.reshape(8, 8, FQ)
        tail = jnp.concatenate([total[:, :, RET:FQ], jnp.zeros((8, 8, 2 * RET - FQ), F32)], axis=2)
        rt_snd[8 * k:8 * k + 8] = jnp.concatenate([total[:, :, 0:RET], tail], axis=1).astype(BF)
        for o in range(8 * k, 8 * k + 8):
            if o == OWN:
                pltpu.make_async_copy(rt_snd.at[o], rt_rcv.at[o], loc_sem.at[1]).start()
                continue
            remote(rt_snd.at[o], rt_rcv.at[o], b_snd.at[k], b_rcv.at[k], (d, peer(BACK[o]))).start()

    pair_c = []
    def weight_grads(q):
        xq = rows[:, q, 0:64, :].reshape(n_rows, FQ)
        gu_mine[q * FQ:(q + 1) * FQ, :] = dot(xq, dgu[...], TN).astype(BF)
        part = pl.ds(q * FQ, FQ)
        c = remote(gu_mine.at[part], gu_theirs.at[part], g_snd.at[q, 0], g_rcv.at[q, 0], partner)
        c.start()
        pair_c.append(c)
        yq = rows[:, q, 64:128, :].reshape(n_rows, FQ)
        gd_mine[q] = dot(sh[...], yq, TN).astype(BF)
        c = remote(gd_mine.at[q], gd_theirs.at[q], g_snd.at[q, 1], g_rcv.at[q, 1], partner)
        c.start()
        pair_c.append(c)

    def merge(q):
        replica = flag_ref[...] == 1
        pair_c[2 * q].wait_recv()
        mine = gu_mine[q * FQ:(q + 1) * FQ, :].astype(F32)
        theirs = gu_theirs[q * FQ:(q + 1) * FQ, :].astype(F32)
        gu_sum[q * FQ:(q + 1) * FQ, :] = (mine + jnp.where(replica, theirs, 0.0)).astype(BF)
        pair_c[2 * q + 1].wait_recv()
        mine = gd_mine[q].astype(F32)
        theirs = gd_theirs[q].astype(F32)
        gd_sum[q] = (mine + jnp.where(replica, theirs, 0.0)).astype(BF)

    relay_source()
    forward(0)
    send_near()
    forward(1)
    share_gates()
    relay(0)
    forward(2)
    relay(1)
    for c in weights_in:
        c.wait()
    for c in gate_c:
        c.wait_recv()
    forward(3)
    relay(2)
    compute(0)
    forward(4)
    relay(3)
    stage2(0)
    stage2(1)
    relay(4)
    compute(1)
    stage3(0)
    stage3(1)
    stage2(2)
    stage2(3)
    compute(2)
    stage3(2)
    stage3(3)
    stage2(4)
    stage2(5)
    compute(3)
    stage3(4)
    stage3(5)
    weight_grads(0)
    stage2(6)
    stage2(7)
    weight_grads(1)
    weight_grads(2)
    stage3(6)
    weight_grads(3)
    stage3(7)
    for q in range(DP):
        merge(q)

    pltpu.make_async_copy(rt_snd.at[OWN], rt_rcv.at[OWN], loc_sem.at[1]).wait()
    for k in range(NCH):
        chunk_wait(rt_rcv, k, b_rcv)
    for k in range(FAR):
        chunk_wait(msg, k, a_snd)
        for c in (to_up[k], to_dn[k], rel_up[k], rel_dn[k]):
            c.wait_send()
    for k in range(FAR, NCH):
        chunk_wait(near_msg, k, a_snd, 8, 8 * FAR)
    for c in src_up + src_dn:
        c.wait_send()
    for k in range(NCH):
        chunk_wait(rt_snd, k, b_snd)
        for c in rs_c[k] + fin_c[k]:
            c.wait_send()
    for c in gate_c:
        c.wait_send()
    each_dp(functools.partial(gates_wait, gt_snd))
    for c in pair_c:
        c.wait_send()


def finish(ret_ref, sel_ref, gu_ref, gd_ref, gt_ref, og_ref, ou_ref, od_ref, sem):
    copies = [
        pltpu.make_async_copy(gu_ref.at[:, pl.ds(0, HQ)], og_ref.at[0], sem.at[0]),
        pltpu.make_async_copy(gu_ref.at[:, pl.ds(HQ, HQ)], ou_ref.at[0], sem.at[1]),
    ]
    for q in range(DP):
        copies.append(pltpu.make_async_copy(gd_ref.at[q], od_ref.at[0, :, pl.ds(q * FQ, FQ)], sem.at[2 + q]))
    for c in copies:
        c.start()
    picks = sel_ref[...].astype(F32).reshape(SLOTS, CAP, TOK)
    none = jnp.zeros_like(picks)
    back = ret_ref[...].reshape(SLOTS * 16, RET)
    low = jnp.concatenate([picks, none], axis=1).reshape(SLOTS * 16, TOK).astype(BF)
    high = jnp.concatenate([none, picks], axis=1).reshape(SLOTS * 16, TOK).astype(BF)
    gt_ref[:, 0:RET] = dot(low, back, TN).astype(BF)
    gt_ref[:, RET:FQ] = dot(high, back, TN)[:, 0:FQ - RET].astype(BF)
    for c in copies:
        c.wait()


def on_device(tokens, grad_out, routes, gates, replicated, w_gate, w_up, w_down):
    vmem = pl.BlockSpec(memory_space=pltpu.VMEM)
    hbm = pl.BlockSpec(memory_space=pl.ANY)
    dma = pltpu.SemaphoreType.DMA
    n_rows = SLOTS * CAP
    results = pl.pallas_call(
        kernel,
        out_shape=(
            pltpu.VMEM((SLOTS, 16, RET), BF),
            pltpu.VMEM((n_rows, TOK), BF),
            pltpu.VMEM((D, 2 * HQ), BF),
            pltpu.VMEM((DP, HQ, FQ), BF),
        ),
        in_specs=[vmem] * 5 + [hbm] * 3,
        out_specs=(vmem,) * 4,
        scratch_shapes=[
            pltpu.VMEM((D, 2 * HQ), BF),
            pltpu.VMEM((HQ, D), BF),
            pltpu.VMEM((DP, 2, TOK, FQ), BF),
            pltpu.VMEM((8 * FAR, 16, FQ), BF),
            pltpu.VMEM((8 * FAR, 16, FQ), BF),
            pltpu.VMEM((8 * NEAR, 16, D), BF),
            pltpu.VMEM((8 * NEAR, 16, D), BF),
            pltpu.VMEM((NCH, DP, 128, FQ), BF),
            pltpu.VMEM((SLOTS, 16, 128), BF),
            pltpu.VMEM((16, 16, 128), BF),
            pltpu.VMEM((DP, 128, 128), BF),
            pltpu.VMEM((n_rows, 2 * HQ), BF),
            pltpu.VMEM((n_rows, HQ), BF),
            pltpu.VMEM((NCH, 64, FQ), BF),
            pltpu.VMEM((NCH, 32, FQ), BF),
            pltpu.VMEM((NCH, 32, FQ), BF),
            pltpu.VMEM((NCH, 64, FQ), F32),
            pltpu.VMEM((NCH, 64, FQ), F32),
            pltpu.VMEM((NCH, 64, FQ), F32),
            pltpu.VMEM((NCH, 2, 64, FQ), BF),
            pltpu.VMEM((NCH, 2, 64, FQ), BF),
            pltpu.VMEM((SLOTS, 16, RET), BF),
            pltpu.VMEM((D, 2 * HQ), BF),
            pltpu.VMEM((DP, HQ, FQ), BF),
            pltpu.VMEM((D, 2 * HQ), BF),
            pltpu.VMEM((DP, HQ, FQ), BF),
            dma((3,)), dma((3,)),
            dma((NCH,)), dma((NCH,)),
            dma((NCH, 2)), dma((NCH, 2)),
            dma((NCH, 2)), dma((NCH, 2)),
            dma((NCH, 2)), dma((NCH, 2)),
            dma((NCH, 2)), dma((NCH, 2)),
            dma((NCH,)), dma((NCH,)),
            dma((DP, 2)), dma((DP, 2)),
            dma((4,)), dma((4,)), dma((2,)), dma((2,)),
            dma((1,)), dma((1,)), dma((3,)), dma((3,)), pltpu.SemaphoreType.REGULAR((2,)),
        ],
        compiler_params=pltpu.CompilerParams(
            collective_id=0, has_side_effects=True, vmem_limit_bytes=VLIM
        ),
        cost_estimate=pl.CostEstimate(flops=8 * 10**9, bytes_accessed=12 * 10**6, transcendentals=0),
    )(
        tokens, grad_out, routes.T, gates.T, replicated.reshape(1, 1),
        w_gate, w_up, w_down,
    )
    return pl.pallas_call(
        finish,
        out_shape=(
            jax.ShapeDtypeStruct((TOK, FQ), BF),
            jax.ShapeDtypeStruct((1, D, HQ), BF),
            jax.ShapeDtypeStruct((1, D, HQ), BF),
            jax.ShapeDtypeStruct((1, HQ, D), BF),
        ),
        in_specs=[vmem] * 4,
        out_specs=(vmem,) + (hbm,) * 3,
        scratch_shapes=[dma((2 + DP,))],
        compiler_params=pltpu.CompilerParams(vmem_limit_bytes=16 * 2**20),
        cost_estimate=pl.CostEstimate(flops=3 * 10**8, bytes_accessed=7 * 10**6, transcendentals=0),
    )(*results)


def solution(mesh):
    return jax.shard_map(
        on_device,
        mesh=mesh,
        in_specs=(
            P("expert", "dp"),
            P("expert", "dp"),
            P("expert", None),
            P("expert", None),
            P("expert"),
            P("expert", None, "dp"),
            P("expert", None, "dp"),
            P("expert", "dp", None),
        ),
        out_specs=(
            P("expert", "dp"),
            P("expert", None, "dp"),
            P("expert", None, "dp"),
            P("expert", "dp", None),
        ),
        check_vma=False,
    )
```

```python
import functools

import jax
import jax.numpy as jnp
from jax import lax
from jax.experimental import pallas as pl
from jax.experimental.pallas import tpu as pltpu
from jax.sharding import PartitionSpec as P

MESH = pl.DeviceIdType.MESH
BF, F32 = jnp.bfloat16, jnp.float32
D, H, DP = 3584, 1024, 4
FQ, HQ = D // DP, H // DP
TOK, CAP, SLOTS = 128, 8, 64
NX, NZ = 4, 8
VLIM = 50 * 2**20
NCH = 8
NPAIR = 4
NEAR = 3
FAR = NCH - NEAR
RET = 512


NEAR_OFFSETS = [(dx, dz, dc) for dx, dz in ((0, 2), (0, -2), (1, 1), (-1, -1)) for dc in (0, 1)]
NEAR_OFFSETS += [(dx, dz, dc) for dx, dz in ((0, 1), (0, -1), (1, -1), (-1, 1)) for dc in (0, 1)]
NEAR_OFFSETS += [(dx, 0, dc) for dx in (0, 1, -1, 2) for dc in (0, 1)]
NEAR_OFFSETS = [(dx % NX, dz % NZ, dc) for dx, dz, dc in NEAR_OFFSETS]
FAR_OFFSETS = [(dx, dz, dc) for dz in range(NZ) for dx in range(NX) for dc in (0, 1)]
FAR_OFFSETS = [o for o in FAR_OFFSETS if o not in NEAR_OFFSETS]
OFFSETS = [o for k in range(FAR) for o in FAR_OFFSETS[k::FAR]] + NEAR_OFFSETS
OWN = OFFSETS.index((0, 0, 0))
BACK = [OFFSETS.index(((-dx) % NX, (-dz) % NZ, dc)) for dx, dz, dc in OFFSETS]


def dot(a, b, dims):
    return lax.dot_general(a, b, ((dims[0], dims[1]), ((), ())), preferred_element_type=F32)


NN, NT, TN = ((1,), (0,)), ((1,), (1,)), ((0,), (0,))


def kernel(
    tok_ref, dy_ref, routes_ref, gates_ref, flag_ref, wg_ref, wu_ref, wd_ref,
    rt_rcv, sel, gu_sum, gd_sum,
    wgu, wdn, full, msg, land, near_msg, near_land, rows, g_msg, g_land, g_rows, dgu, sh,
    rs_snd, rs_a, rs_b, p_up, p_dn, p_own, fin_snd, fin_rcv, rt_snd,
    gu_mine, gd_mine, gu_theirs, gd_theirs,
    w_sem, loc_sem, a_snd, a_rcv, y_snd, y_rcv, r_snd, r_rcv, q_snd, q_rcv, f_snd, f_rcv,
    b_snd, b_rcv, g_snd, g_rcv, t_snd, t_rcv, u_snd, u_rcv, gt_snd, gt_rcv, gs_snd, gs_rcv, sync,
):
    d = lax.axis_index("dp")
    e = lax.axis_index("expert")
    x0, z0, c0 = e // 16, (e // 2) % NZ, e % 2
    up, dn, op = (d + 1) % DP, (d + 3) % DP, (d + 2) % DP

    def peer(o):
        dx, dz, dc = OFFSETS[o]
        return ((x0 + dx) % NX * NZ + (z0 + dz) % NZ) * 2 + (c0 + dc) % 2

    def remote(src, dst, s, r, dev):
        return pltpu.make_async_remote_copy(src, dst, s, r, device_id=dev, device_id_type=MESH)

    weights_in = [
        pltpu.make_async_copy(wg_ref.at[0], wgu.at[:, pl.ds(0, HQ)], w_sem.at[0]),
        pltpu.make_async_copy(wu_ref.at[0], wgu.at[:, pl.ds(HQ, HQ)], w_sem.at[1]),
        pltpu.make_async_copy(wd_ref.at[0], wdn, w_sem.at[2]),
    ]
    for c in weights_in:
        c.start()

    barrier = pltpu.get_barrier_semaphore()
    def greet(sem, devices):
        for dev in devices:
            pl.semaphore_signal(sem, inc=1, device_id=dev, device_id_type=MESH)

    along_x = [(d, ((x0 + i) % NX * NZ + z0) * 2 + c0) for i in range(1, NX)]
    along_z = [(d, (x0 * NZ + (z0 + i) % NZ) * 2 + c0) for i in range(1, NZ)]
    partner = (d, e + 1 - 2 * c0)
    along_y = [((d + i) % DP, e) for i in range(1, DP)]
    greet(barrier, along_y + along_z + along_x + [partner])

    io = lax.broadcasted_iota(jnp.int32, (SLOTS, TOK), 0)
    slot = jnp.zeros((SLOTS, TOK), jnp.int32)
    for o in range(SLOTS):
        slot = jnp.where(io == o, peer(o), slot)
    on0 = routes_ref[0:1, :] == slot
    on1 = routes_ref[1:2, :] == slot
    hot0 = on0.astype(F32)
    hot1 = on1.astype(F32)
    before = (
        lax.broadcasted_iota(jnp.int32, (TOK, TOK), 0) < lax.broadcasted_iota(jnp.int32, (TOK, TOK), 1)
    ).astype(BF)
    rank0 = dot(hot0.astype(BF), before, NN)
    rank1 = dot(hot1.astype(BF), before, NN) + jnp.sum(hot0, axis=1, keepdims=True)
    rank0 = jnp.where(on0, rank0, -1.0).astype(BF)
    rank1 = jnp.where(on1, rank1, -1.0).astype(BF)
    n_rows = SLOTS * CAP
    ui = lax.broadcasted_iota(jnp.int32, (n_rows, SLOTS), 0)
    spread = ((ui >> 3) == lax.broadcasted_iota(jnp.int32, (n_rows, SLOTS), 1)).astype(BF)
    place = (lax.broadcasted_iota(jnp.int32, (n_rows, TOK), 0) & 7).astype(F32)
    sel0 = (dot(spread, rank0, NN) == place).astype(F32)
    sel1 = (dot(spread, rank1, NN) == place).astype(F32)
    sel[...] = (sel0 + sel1).astype(BF)
    gates = gates_ref[...].astype(F32)
    gate_of = (sel0 * gates[0:1, :] + sel1 * gates[1:2, :]).astype(BF)
    gates_of = dot(gate_of, jnp.ones((TOK, 128), BF), NN).reshape(SLOTS, CAP, 128)
    g_msg[...] = jnp.concatenate([gates_of, gates_of], axis=1).astype(BF)

    pl.semaphore_wait(barrier, DP + NZ + NX - 3 + 1)
    greet(sync.at[0], along_x)

    src_up = [
        remote(tok_ref, full.at[d, 0], t_snd.at[0], t_rcv.at[0], (up, e)),
        remote(dy_ref, full.at[d, 1], t_snd.at[1], t_rcv.at[1], (up, e)),
    ]
    src_dn = [
        remote(dy_ref, full.at[d, 1], t_snd.at[2], t_rcv.at[2], (dn, e)),
        remote(tok_ref, full.at[d, 0], t_snd.at[3], t_rcv.at[3], (dn, e)),
    ]
    for i in range(2):
        src_up[i].start()
        src_dn[i].start()

    def pack(k, out, at, lane, xs, ys):
        s = sel[k * 64:(k + 1) * 64, :]
        xk = dot(s, xs, NN).reshape(8, 8, FQ)
        yk = dot(s, ys, NN).reshape(8, 8, FQ)
        lanes = pl.ds(lane, FQ) if isinstance(lane, int) else pl.ds(pl.multiple_of(lane, 128), FQ)
        out[at:at + 8, :, lanes] = jnp.concatenate([xk, yk], axis=1).astype(BF)

    def send(k, src, dst, base):
        for o in range(8 * k, 8 * k + 8):
            if o == OWN:
                pltpu.make_async_copy(src.at[o - base], dst.at[o - base], loc_sem.at[0]).start()
                continue
            remote(src.at[o - base], dst.at[o - base], a_snd.at[k], a_rcv.at[k], (d, peer(o))).start()

    def each_dp(act):
        for p in range(DP):
            pl.when(d == p)(functools.partial(act, p))

    def send_gates(p):
        for o in range(16 * p, 16 * p + 16):
            if o == OWN:
                pltpu.make_async_copy(g_msg.at[o], g_land.at[o - 16 * p], loc_sem.at[2]).start()
                continue
            remote(g_msg.at[o], g_land.at[o - 16 * p], gt_snd.at[0], gt_rcv.at[0], (d, peer(o))).start()

    def gates_wait(sem, p):
        n = 15 if 16 * p <= OWN < 16 * p + 16 else 16
        block = g_land.at[pl.ds(0, n)]
        pltpu.make_async_copy(block, block, sem.at[0]).wait()

    def take_gates(p):
        if 16 * p <= OWN < 16 * p + 16:
            pltpu.make_async_copy(g_msg.at[OWN], g_land.at[OWN - 16 * p], loc_sem.at[2]).wait()
        gates_wait(gt_rcv, p)

    def share_gates():
        each_dp(take_gates)
        g_rows[d] = g_land[...].astype(F32)[:, 0:8, :].reshape(128, 128).astype(BF)
        for i, to in enumerate((up, op, dn)):
            gate_c.append(remote(g_rows.at[d], g_rows.at[d], gs_snd.at[i], gs_rcv.at[i], (to, e)))
            gate_c[i].start()

    gate_c = []
    for k in range(FAR):
        pack(k, msg, 8 * k, 0, tok_ref[...], dy_ref[...])
        if k == 0:
            pl.semaphore_wait(sync.at[0], NX - 1)
            greet(sync.at[1], [partner])
            pl.semaphore_wait(sync.at[1], 1)
            each_dp(send_gates)
        send(k, msg, land, 0)

    def relay_source():
        src_up[0].wait_recv()
        part = full.at[dn, 0]
        src_up.append(remote(part, part, u_snd.at[0], u_rcv.at[0], (up, e)))
        src_up[2].start()
        src_dn[0].wait_recv()
        part = full.at[up, 1]
        src_dn.append(remote(part, part, u_snd.at[1], u_rcv.at[1], (dn, e)))
        src_dn[2].start()

    def send_near():
        for c in (src_up[1], src_dn[1], src_up[2], src_dn[2]):
            c.wait_recv()
        full[d, 0] = tok_ref[...]
        full[d, 1] = dy_ref[...]
        for k in range(FAR, NCH):
            at = 8 * (k - FAR)
            for q in range(DP):
                pack(k, near_msg, at, q * FQ, full[q, 0], full[q, 1])
            send(k, near_msg, near_land, 8 * FAR)

    def chunk_wait(buf, k, sem, per=8, base=0):
        lo, n = per * k, per
        if lo <= OWN < lo + per:
            n = per - 1
        block = buf.at[pl.ds(lo - base, n)]
        pltpu.make_async_copy(block, block, sem.at[k]).wait()

    to_up, to_dn, rel_up, rel_dn = {}, {}, {}, {}

    def unpack(k, block, lane, q):
        rows[k, q, 0:64, :] = block[:, 0:8, lane:lane + FQ].reshape(64, FQ).astype(BF)
        rows[k, q, 64:128, :] = block[:, 8:16, lane:lane + FQ].reshape(64, FQ).astype(BF)

    def forward(k):
        chunk_wait(land, k, a_rcv)
        block = land[k * 8:(k + 1) * 8].astype(F32)
        unpack(k, block, 0, d)
        mine = rows.at[k, d]
        to_up[k] = remote(mine, mine, y_snd.at[k, 0], y_rcv.at[k, 0], (up, e))
        to_dn[k] = remote(mine, mine, y_snd.at[k, 1], y_rcv.at[k, 1], (dn, e))
        to_up[k].start()
        to_dn[k].start()

    def take_near(k):
        if 8 * k <= OWN < 8 * k + 8:
            at = OWN - 8 * FAR
            pltpu.make_async_copy(near_msg.at[at], near_land.at[at], loc_sem.at[0]).wait()
        chunk_wait(near_land, k, a_rcv, 8, 8 * FAR)
        at = 8 * (k - FAR)
        for q in range(DP):
            block = near_land[at:at + 8, :, q * FQ:(q + 1) * FQ].astype(F32)
            unpack(k, block, 0, q)

    def relay(k):
        to_up[k].wait_recv()
        part = rows.at[k, dn, pl.ds(0, 64)]
        rel_up[k] = remote(part, part, r_snd.at[k, 0], r_rcv.at[k, 0], (up, e))
        rel_up[k].start()
        to_dn[k].wait_recv()
        part = rows.at[k, up, pl.ds(64, 64)]
        rel_dn[k] = remote(part, part, r_snd.at[k, 1], r_rcv.at[k, 1], (dn, e))
        rel_dn[k].start()

    def row_part(p, q):
        rng = pl.ds(pl.multiple_of(q * FQ, FQ), FQ)
        return dot(dgu[p * 128:(p + 1) * 128, :], wgu[rng, :], NT)

    rs_c = {}

    def compute(p):
        for k in (2 * p, 2 * p + 1):
            if k < FAR:
                rel_up[k].wait_recv()
                rel_dn[k].wait_recv()
            else:
                take_near(k)
        pre = jnp.zeros((128, 2 * HQ), F32)
        dh = jnp.zeros((128, HQ), F32)
        for q in range(DP):
            xq = rows[2 * p:2 * p + 2, q, 0:64, :].reshape(128, FQ)
            yq = rows[2 * p:2 * p + 2, q, 64:128, :].reshape(128, FQ)
            pre = pre + dot(xq, wgu[q * FQ:(q + 1) * FQ, :], NN)
            dh = dh + dot(yq, wdn[:, q * FQ:(q + 1) * FQ], NT)
        g = g_rows[p].astype(F32)
        g = jnp.concatenate([g, g], axis=1)
        pg, pu = pre[:, 0:HQ], pre[:, HQ:]
        sig = jax.nn.sigmoid(pg)
        act = pg * sig
        dh = g * dh
        span = slice(p * 128, (p + 1) * 128)
        sh[span, :] = (g * act * pu).astype(BF)
        dgu[span, 0:HQ] = (dh * pu * sig * (1.0 + pg * (1.0 - sig))).astype(BF)
        dgu[span, HQ:] = (dh * act).astype(BF)
        rs_snd[2 * p:2 * p + 2] = row_part(p, op).astype(BF).reshape(2, 64, FQ)
        for k in (2 * p, 2 * p + 1):
            rs_c[k] = (
                remote(rs_snd.at[k, pl.ds(0, 32)], rs_a.at[k], q_snd.at[k, 0], q_rcv.at[k, 0], (up, e)),
                remote(rs_snd.at[k, pl.ds(32, 32)], rs_b.at[k], q_snd.at[k, 1], q_rcv.at[k, 1], (dn, e)),
            )
            for c in rs_c[k]:
                c.start()
        p_up[2 * p:2 * p + 2] = row_part(p, up).reshape(2, 64, FQ)
        p_dn[2 * p:2 * p + 2] = row_part(p, dn).reshape(2, 64, FQ)
        p_own[2 * p:2 * p + 2] = row_part(p, d).reshape(2, 64, FQ)

    fin_c = {}

    def stage2(k):
        rs_c[k][0].wait_recv()
        fin_snd[k, 0, 0:32, :] = (p_up[k, 0:32, :] + rs_a[k].astype(F32)).astype(BF)
        fin_snd[k, 0, 32:64, :] = p_up[k, 32:64, :].astype(BF)
        first = remote(fin_snd.at[k, 0], fin_rcv.at[k, 0], f_snd.at[k, 0], f_rcv.at[k, 0], (up, e))
        first.start()
        rs_c[k][1].wait_recv()
        fin_snd[k, 1, 0:32, :] = p_dn[k, 0:32, :].astype(BF)
        fin_snd[k, 1, 32:64, :] = (p_dn[k, 32:64, :] + rs_b[k].astype(F32)).astype(BF)
        second = remote(fin_snd.at[k, 1], fin_rcv.at[k, 1], f_snd.at[k, 1], f_rcv.at[k, 1], (dn, e))
        second.start()
        fin_c[k] = (first, second)

    def stage3(k):
        fin_c[k][0].wait_recv()
        fin_c[k][1].wait_recv()
        total = p_own[k] + fin_rcv[k, 0].astype(F32) + fin_rcv[k, 1].astype(F32)
        total = total.reshape(8, 8, FQ)
        tail = jnp.concatenate([total[:, :, RET:FQ], jnp.zeros((8, 8, 2 * RET - FQ), F32)], axis=2)
        rt_snd[8 * k:8 * k + 8] = jnp.concatenate([total[:, :, 0:RET], tail], axis=1).astype(BF)
        for o in range(8 * k, 8 * k + 8):
            if o == OWN:
                pltpu.make_async_copy(rt_snd.at[o], rt_rcv.at[o], loc_sem.at[1]).start()
                continue
            remote(rt_snd.at[o], rt_rcv.at[o], b_snd.at[k], b_rcv.at[k], (d, peer(BACK[o]))).start()

    pair_c = []
    def weight_grads(q):
        xq = rows[:, q, 0:64, :].reshape(n_rows, FQ)
        gu_mine[q * FQ:(q + 1) * FQ, :] = dot(xq, dgu[...], TN).astype(BF)
        part = pl.ds(q * FQ, FQ)
        c = remote(gu_mine.at[part], gu_theirs.at[part], g_snd.at[q, 0], g_rcv.at[q, 0], partner)
        c.start()
        pair_c.append(c)
        yq = rows[:, q, 64:128, :].reshape(n_rows, FQ)
        gd_mine[q] = dot(sh[...], yq, TN).astype(BF)
        c = remote(gd_mine.at[q], gd_theirs.at[q], g_snd.at[q, 1], g_rcv.at[q, 1], partner)
        c.start()
        pair_c.append(c)

    def merge(q):
        replica = flag_ref[0] == 1
        pair_c[2 * q].wait_recv()
        mine = gu_mine[q * FQ:(q + 1) * FQ, :].astype(F32)
        theirs = gu_theirs[q * FQ:(q + 1) * FQ, :].astype(F32)
        gu_sum[q * FQ:(q + 1) * FQ, :] = (mine + jnp.where(replica, theirs, 0.0)).astype(BF)
        pair_c[2 * q + 1].wait_recv()
        mine = gd_mine[q].astype(F32)
        theirs = gd_theirs[q].astype(F32)
        gd_sum[q] = (mine + jnp.where(replica, theirs, 0.0)).astype(BF)

    relay_source()
    forward(0)
    send_near()
    forward(1)
    share_gates()
    relay(0)
    forward(2)
    relay(1)
    for c in weights_in:
        c.wait()
    for c in gate_c:
        c.wait_recv()
    forward(3)
    relay(2)
    compute(0)
    forward(4)
    relay(3)
    stage2(0)
    stage2(1)
    relay(4)
    compute(1)
    stage3(0)
    stage3(1)
    stage2(2)
    stage2(3)
    compute(2)
    stage3(2)
    stage3(3)
    stage2(4)
    stage2(5)
    compute(3)
    stage3(4)
    stage3(5)
    weight_grads(0)
    stage2(6)
    stage2(7)
    weight_grads(1)
    weight_grads(2)
    weight_grads(3)
    stage3(6)
    merge(0)
    merge(1)
    stage3(7)
    merge(2)
    merge(3)

    pltpu.make_async_copy(rt_snd.at[OWN], rt_rcv.at[OWN], loc_sem.at[1]).wait()
    for k in range(NCH):
        chunk_wait(rt_rcv, k, b_rcv)
    for k in range(FAR):
        chunk_wait(msg, k, a_snd)
        for c in (to_up[k], to_dn[k], rel_up[k], rel_dn[k]):
            c.wait_send()
    for k in range(FAR, NCH):
        chunk_wait(near_msg, k, a_snd, 8, 8 * FAR)
    for c in src_up + src_dn:
        c.wait_send()
    for k in range(NCH):
        chunk_wait(rt_snd, k, b_snd)
        for c in rs_c[k] + fin_c[k]:
            c.wait_send()
    for c in gate_c:
        c.wait_send()
    each_dp(functools.partial(gates_wait, gt_snd))
    for c in pair_c:
        c.wait_send()


def finish(ret_ref, sel_ref, gu_ref, gd_ref, gt_ref, og_ref, ou_ref, od_ref, sem):
    copies = [
        pltpu.make_async_copy(gu_ref.at[:, pl.ds(0, HQ)], og_ref.at[0], sem.at[0]),
        pltpu.make_async_copy(gu_ref.at[:, pl.ds(HQ, HQ)], ou_ref.at[0], sem.at[1]),
    ]
    for q in range(DP):
        copies.append(pltpu.make_async_copy(gd_ref.at[q], od_ref.at[0, :, pl.ds(q * FQ, FQ)], sem.at[2 + q]))
    for c in copies:
        c.start()
    picks = sel_ref[...].astype(F32).reshape(SLOTS, CAP, TOK)
    none = jnp.zeros_like(picks)
    back = ret_ref[...].reshape(SLOTS * 16, RET)
    low = jnp.concatenate([picks, none], axis=1).reshape(SLOTS * 16, TOK).astype(BF)
    high = jnp.concatenate([none, picks], axis=1).reshape(SLOTS * 16, TOK).astype(BF)
    gt_ref[:, 0:RET] = dot(low, back, TN).astype(BF)
    gt_ref[:, RET:FQ] = dot(high, back, TN)[:, 0:FQ - RET].astype(BF)
    for c in copies:
        c.wait()


def on_device(tokens, grad_out, routes, gates, replicated, w_gate, w_up, w_down):
    vmem = pl.BlockSpec(memory_space=pltpu.VMEM)
    hbm = pl.BlockSpec(memory_space=pl.ANY)
    dma = pltpu.SemaphoreType.DMA
    n_rows = SLOTS * CAP
    results = pl.pallas_call(
        kernel,
        out_shape=(
            pltpu.VMEM((SLOTS, 16, RET), BF),
            pltpu.VMEM((n_rows, TOK), BF),
            pltpu.VMEM((D, 2 * HQ), BF),
            pltpu.VMEM((DP, HQ, FQ), BF),
        ),
        in_specs=[vmem] * 4 + [pl.BlockSpec(memory_space=pltpu.SMEM)] + [hbm] * 3,
        out_specs=(vmem,) * 4,
        scratch_shapes=[
            pltpu.VMEM((D, 2 * HQ), BF),
            pltpu.VMEM((HQ, D), BF),
            pltpu.VMEM((DP, 2, TOK, FQ), BF),
            pltpu.VMEM((8 * FAR, 16, FQ), BF),
            pltpu.VMEM((8 * FAR, 16, FQ), BF),
            pltpu.VMEM((8 * NEAR, 16, D), BF),
            pltpu.VMEM((8 * NEAR, 16, D), BF),
            pltpu.VMEM((NCH, DP, 128, FQ), BF),
            pltpu.VMEM((SLOTS, 16, 128), BF),
            pltpu.VMEM((16, 16, 128), BF),
            pltpu.VMEM((DP, 128, 128), BF),
            pltpu.VMEM((n_rows, 2 * HQ), BF),
            pltpu.VMEM((n_rows, HQ), BF),
            pltpu.VMEM((NCH, 64, FQ), BF),
            pltpu.VMEM((NCH, 32, FQ), BF),
            pltpu.VMEM((NCH, 32, FQ), BF),
            pltpu.VMEM((NCH, 64, FQ), F32),
            pltpu.VMEM((NCH, 64, FQ), F32),
            pltpu.VMEM((NCH, 64, FQ), F32),
            pltpu.VMEM((NCH, 2, 64, FQ), BF),
            pltpu.VMEM((NCH, 2, 64, FQ), BF),
            pltpu.VMEM((SLOTS, 16, RET), BF),
            pltpu.VMEM((D, 2 * HQ), BF),
            pltpu.VMEM((DP, HQ, FQ), BF),
            pltpu.VMEM((D, 2 * HQ), BF),
            pltpu.VMEM((DP, HQ, FQ), BF),
            dma((3,)), dma((3,)),
            dma((NCH,)), dma((NCH,)),
            dma((NCH, 2)), dma((NCH, 2)),
            dma((NCH, 2)), dma((NCH, 2)),
            dma((NCH, 2)), dma((NCH, 2)),
            dma((NCH, 2)), dma((NCH, 2)),
            dma((NCH,)), dma((NCH,)),
            dma((DP, 2)), dma((DP, 2)),
            dma((4,)), dma((4,)), dma((2,)), dma((2,)),
            dma((1,)), dma((1,)), dma((3,)), dma((3,)), pltpu.SemaphoreType.REGULAR((2,)),
        ],
        compiler_params=pltpu.CompilerParams(
            collective_id=0, has_side_effects=True, vmem_limit_bytes=VLIM
        ),
        cost_estimate=pl.CostEstimate(flops=8 * 10**9, bytes_accessed=12 * 10**6, transcendentals=0),
    )(
        tokens, grad_out, routes.T, gates.T, replicated,
        w_gate, w_up, w_down,
    )
    return pl.pallas_call(
        finish,
        out_shape=(
            jax.ShapeDtypeStruct((TOK, FQ), BF),
            jax.ShapeDtypeStruct((1, D, HQ), BF),
            jax.ShapeDtypeStruct((1, D, HQ), BF),
            jax.ShapeDtypeStruct((1, HQ, D), BF),
        ),
        in_specs=[vmem] * 4,
        out_specs=(vmem,) + (hbm,) * 3,
        scratch_shapes=[dma((2 + DP,))],
        compiler_params=pltpu.CompilerParams(vmem_limit_bytes=16 * 2**20),
        cost_estimate=pl.CostEstimate(flops=3 * 10**8, bytes_accessed=7 * 10**6, transcendentals=0),
    )(*results)


def solution(mesh):
    return jax.shard_map(
        on_device,
        mesh=mesh,
        in_specs=(
            P("expert", "dp"),
            P("expert", "dp"),
            P("expert", None),
            P("expert", None),
            P("expert"),
            P("expert", None, "dp"),
            P("expert", None, "dp"),
            P("expert", "dp", None),
        ),
        out_specs=(
            P("expert", "dp"),
            P("expert", None, "dp"),
            P("expert", None, "dp"),
            P("expert", "dp", None),
        ),
        check_vma=False,
    )
```
